128 devices in a mesh: gx: 4 (over y_hi, core), gy: 32 (over y_lo, z, x).
Axes of the slice: x: 4, y: 4 (y_hi: 2, y_lo: 2; y = y_hi * 2 + y_lo), z: 4, core: 2. Of those that a mesh axis runs over, the one named last changes fastest.
Arguments:
- inputs: bfloat16 [256, 256, 384], P('gx', 'gy'), may hold values from -6 to 6
- norm_gains: float32 [4, 384], replicated, may hold values from 0.5 to 1.5
- weights: bfloat16 [4, 3456, 384], replicated, may hold values from -0.109375 to 0.109375
- cotangent: float32 [256, 256, 384], P('gx', 'gy'), may hold values from -6 to 6
Outputs:
- outputs: float32 [256, 256, 384], P('gx', 'gy')
- input_grad: float32 [256, 256, 384], P('gx', 'gy')
- weight_grads: float32 [4, 1327104], P(None, ('gx', 'gy'))
The draws below stay inside these ranges and needn't reach their ends.
All inputs are finite; a program needn't handle non-finite values.
Results may differ from the reference program's by a relative error of at most 0.0048.
Values may be sent and summed in bfloat16 or wider, within the bound.
A program may use at most 192 MiB of HBM per device.

```python
import math
import jax
import jax.numpy as jnp
from jax import lax

CH = 384
BLOCKS = 4
HEIGHT = 256
WIDTH = 256


def levels(rng, shape, cuts, smallest, high):
    gain = 1.0
    for dim, shards_of in cuts:
        heights = jax.random.uniform(jax.random.fold_in(jax.random.fold_in(rng, 6), dim), (shards_of,), jnp.float32, smallest / len(cuts), high / len(cuts))
        gain = gain * jnp.repeat(jnp.exp(heights), shape[dim] // shards_of).reshape((-1,) + (1,) * (len(shape) - 1 - dim))
    return gain


def normal_values(key, shape, width, bound, pieces=(), held_as=jnp.bfloat16):
    entries = width * jax.random.normal(key, shape, jnp.float32)
    if pieces:
        entries = entries * levels(key, shape, pieces, -0.22, 0.18)
    return jnp.clip(entries, -bound, bound).astype(held_as)


def setup_inputs(seed: int = 0) -> dict:
    seeds = jax.random.split(jax.random.key(seed), 5)
    return {
        "inputs": normal_values(seeds[0], (HEIGHT, WIDTH, CH), 1.0, 6.0, ((0, 4), (1, 32))),
        "norm_gains": jnp.clip(1.0 + 0.1 * jax.random.normal(seeds[1], (BLOCKS, CH), jnp.float32), 0.5, 1.5),
        "weights": normal_values(seeds[2], (BLOCKS, 9 * CH, CH), (9 * CH) ** -0.5, 0.109375),
        "cotangent": normal_values(seeds[3], (HEIGHT, WIDTH, CH), 1.0, 6.0, ((0, 4), (1, 32)), jnp.float32),
    }


DILATIONS = (1, 4, 32, 128)
OFFSETS = tuple(((row_step, col_step) for row_step in (-1, 0, 1) for col_step in (-1, 0, 1)))
EPSILON = 1e-05

def norm_act(stream, gain_row):
    average = lax.optimization_barrier(jnp.mean(stream, axis=-1, keepdims=True))
    centred = stream - average
    spread = lax.optimization_barrier(jnp.mean(centred * centred, axis=-1, keepdims=True))
    return jax.nn.gelu(centred * lax.rsqrt(spread + EPSILON) * gain_row)

def local_move(source, amount, dim_index):
    extent = source.shape[dim_index]
    if amount == 0:
        return source
    if abs(amount) >= extent:
        return jnp.zeros_like(source)
    leading = max(-amount, 0)
    trailing = max(amount, 0)
    retained = lax.slice_in_dim(source, trailing, extent - leading, axis=dim_index)
    widths = [(0, 0)] * source.ndim
    widths[dim_index] = (leading, trailing)
    return jnp.pad(retained, widths)

def shifted(source, row_cells, col_cells):
    return local_move(local_move(source, row_cells, 0), col_cells, 1)

def reference(inputs, norm_gains, weights, cotangent):
    stream = inputs.astype(jnp.float32)
    saved = []
    for block_index in range(BLOCKS):
        dilation = DILATIONS[block_index]
        saved.append(stream)
        acted = norm_act(stream, norm_gains[block_index]).astype(jnp.bfloat16)
        update = jnp.zeros((HEIGHT * WIDTH, CH), jnp.float32)
        for tap_index, (row_step, col_step) in enumerate(OFFSETS):
            moved = shifted(acted, row_step * dilation, col_step * dilation).reshape(HEIGHT * WIDTH, CH)
            kernel = weights[block_index, tap_index * CH:(tap_index + 1) * CH]
            update = update + jnp.dot(moved, kernel, preferred_element_type=jnp.float32)
        stream = stream + update.reshape(HEIGHT, WIDTH, CH)
    outputs = stream
    scale = 1.0 / math.sqrt(HEIGHT * WIDTH)
    grad = cotangent
    collected = [None] * BLOCKS
    for block_index in range(BLOCKS - 1, -1, -1):
        dilation = DILATIONS[block_index]
        gain_row = norm_gains[block_index]
        acted = norm_act(saved[block_index], gain_row).astype(jnp.bfloat16)
        g_out = grad.astype(jnp.bfloat16)
        flat_grad = g_out.reshape(HEIGHT * WIDTH, CH)
        tap_grads = []
        d_act = jnp.zeros((HEIGHT * WIDTH, CH), jnp.float32)
        for tap_index, (row_step, col_step) in enumerate(OFFSETS):
            moved = shifted(acted, row_step * dilation, col_step * dilation).reshape(HEIGHT * WIDTH, CH)
            tap_grads.append(lax.dot_general(moved, flat_grad, (((0,), (0,)), ((), ())), preferred_element_type=jnp.float32))
            back_taps = shifted(g_out, -row_step * dilation, -col_step * dilation).reshape(HEIGHT * WIDTH, CH)
            kernel = weights[block_index, tap_index * CH:(tap_index + 1) * CH]
            d_act = d_act + jnp.dot(back_taps, kernel.T, preferred_element_type=jnp.float32)
        collected[block_index] = jnp.concatenate(tap_grads, axis=0).reshape(-1) * scale
        _, pullback = jax.vjp(lambda state_in: norm_act(state_in, gain_row), saved[block_index])
        grad = grad + pullback(d_act.reshape(HEIGHT, WIDTH, CH))[0]
    return (outputs, grad, jnp.stack(collected))
```

```python
import math

import jax
import jax.numpy as jnp
from jax import lax
from jax.experimental import pallas as pl
from jax.experimental.pallas import tpu as pltpu
from jax.sharding import PartitionSpec as P

F32 = jnp.float32
BF16 = jnp.bfloat16
MESH = pl.DeviceIdType.MESH
CH = 384
ROWS, COLS = 64, 8
CELLS = ROWS * COLS
TAPS = tuple((r, c) for r in (-1, 0, 1) for c in (-1, 0, 1))
EPSILON = 1e-05
ROOT = math.sqrt(2.0 / math.pi)
CUBIC = 0.044715
PITCH = 24
DIRS = ((0, -1), (0, 1), (-1, 0), (1, 0), (-1, -1), (-1, 1), (1, -1), (1, 1))
CHUNK = 27
ORDERS = (("x", "y", "z"), ("y", "z", "x"), ("z", "x", "y"))


def aligned(value, step):
    return value if isinstance(value, int) else pl.multiple_of(value, step)


def rows(start, size, step=16):
    return pl.ds(aligned(start, step), size)


def normed(stream):
    average = jnp.mean(stream, axis=-1, keepdims=True)
    centred = stream - average
    spread = jnp.mean(centred * centred, axis=-1, keepdims=True)
    inverse = lax.rsqrt(spread + EPSILON)
    return centred * inverse, inverse


def gelu(u):
    return 0.5 * u * (1.0 + jnp.tanh(ROOT * (u + CUBIC * (u * u * u))))


def gelu_slope(u):
    square = u * u
    t = jnp.tanh(ROOT * (u + CUBIC * (square * u)))
    return 0.5 * (1.0 + t) + 0.5 * u * (1.0 - t * t) * (ROOT * (1.0 + 3.0 * CUBIC * square))


def pulled(stream, gain, d_act):
    unit, inverse = normed(stream)
    d_unit = d_act * gelu_slope(unit * gain) * gain
    first = jnp.mean(d_unit, axis=-1, keepdims=True)
    second = jnp.mean(d_unit * unit, axis=-1, keepdims=True)
    return inverse * (d_unit - first - unit * second)


def strip_rows(d):
    return (ROWS * d, ROWS * d, max(COLS * d, 16), max(COLS * d, 16))


def kernel(
    x_ref, gains, w_hbm, cot, out, ig, wg_out,
    W, S, D, AT, F, V, U, G, SB, R0, L1, L2, L3, AS, AL, HS, HL,
    w_sem, hs_sem, hr_sem, as_sem, ar_sem, rs_sem, rr_sem,
):
    gx, gy = lax.axis_index("gx"), lax.axis_index("gy")
    core, y = gx % 2, (gx // 2) * 2 + gy // 16
    z, x = (gy // 4) % 4, gy % 4
    here = {"x": x, "y": y, "z": z}
    me = gx * 8 + gy // 4

    def device(core_of, at):
        return ((at["y"] // 2) * 2 + core_of, (at["y"] % 2) * 16 + at["z"] * 4 + at["x"])

    def plane(q):
        return (q // 8, (q % 8) * 4 + x)

    def exists(direction):
        r, c = gx + direction[0], gy + direction[1]
        return (r >= 0) & (r < 4) & (c >= 0) & (c < 32)

    barrier = pltpu.get_barrier_semaphore()

    def greet(target):
        pl.semaphore_signal(barrier, inc=1, device_id=target, device_id_type=MESH)

    @pl.loop(1, 32)
    def _(step):
        greet(plane((me + step) % 32))

    for step in (1, 2, 3):
        greet(device(core, {**here, "x": (x + step) % 4}))
    greeted = 34
    for direction in DIRS:
        there = exists(direction)

        @pl.when(there)
        def _(direction=direction):
            greet((gx + direction[0], gy + direction[1]))

        greeted = greeted + there.astype(jnp.int32)

    loads = []
    for k in range(4):
        loads.append(pltpu.make_async_copy(w_hbm.at[k], W.at[k], w_sem.at[k]))
        loads[k].start()

    def padded(at):
        return jnp.concatenate([F[p, at, :] for p in range(3)], axis=1)

    def pad_put(at, values):
        for p in range(3):
            F[p, at, :] = values[:, p * 128 : (p + 1) * 128]

    def halo_copy(slot, d, index):
        sizes = strip_rows(d)
        source = (0, 1, 2, 3, 2, 2, 3, 3)[index]
        size = sizes[source]
        starts = [sum(sizes[:i]) for i in range(4)]
        landed = (0, 1, 2, 3, 2, 2, 3, 3)
        lands = [sum(sizes[landed[j]] for j in range(i)) for i in range(8)]
        direction = DIRS[index]
        opposite = DIRS.index((-direction[0], -direction[1]))
        return pltpu.make_async_remote_copy(
            src_ref=HS.at[slot, pl.ds(starts[source], size)],
            dst_ref=HL.at[slot, pl.ds(lands[opposite], size)],
            send_sem=hs_sem.at[slot, index],
            recv_sem=hr_sem.at[slot, opposite],
            device_id=(gx + direction[0], gy + direction[1]),
            device_id_type=MESH,
        )

    def halo_send(slot, d):
        sizes = strip_rows(d)
        at = 0
        for first in (0, COLS - d):
            for j in range(d):
                column = padded(pl.ds(d * PITCH + 8 + first + j, ROWS, stride=PITCH))
                HS[slot, pl.ds(at + j * ROWS, ROWS), :] = column.astype(BF16)
            at += ROWS * d
        count = sizes[2] // COLS
        for first in (0, ROWS - count):
            for i in range(0, count, 2):
                pair = [padded(pl.ds((d + first + i + n) * PITCH + 8, 8)) for n in (0, 1)]
                HS[slot, pl.ds(at + i * 8, 16), :] = jnp.concatenate(pair, axis=0).astype(BF16)
            at += sizes[2]
        for index, direction in enumerate(DIRS):

            @pl.when(exists(direction))
            def _(index=index):
                halo_copy(slot, d, index).start()

    def halo_receive(slot, d):
        sizes = strip_rows(d)
        landed = (0, 1, 2, 3, 2, 2, 3, 3)
        lands = [sum(sizes[landed[j]] for j in range(i)) for i in range(8)]
        count = sizes[2] // COLS
        for index, direction in enumerate(DIRS):
            there = exists(direction)

            def put(values, index=index, direction=direction):
                if direction[0] == 0:
                    first = 8 - d if direction[1] < 0 else 16
                    for j in range(d):
                        pad_put(pl.ds(d * PITCH + first + j, ROWS, stride=PITCH), values(j * ROWS, ROWS))
                else:
                    first = 0 if direction[0] < 0 else d + ROWS
                    skip = count - d if direction[0] < 0 else 0
                    for i in range(0, count, 2):
                        both = values(i * 8, 16)
                        for n in (0, 1):
                            row = i + n - skip
                            if 0 <= row < d:
                                start = (first + row) * PITCH + 8 + 8 * direction[1]
                                pad_put(pl.ds(start, 8), both[n * 8 : n * 8 + 8])

            @pl.when(there)
            def _(index=index, direction=direction, put=put):
                opposite = DIRS.index((-direction[0], -direction[1]))
                halo_copy(slot, d, opposite).wait_recv()
                put(lambda at, size: HL[slot, pl.ds(lands[index] + at, size), :].astype(F32))

            @pl.when(jnp.logical_not(there))
            def _(put=put):
                put(lambda at, size: jnp.zeros((size, CH), F32))

    def near_versions(d):
        @pl.loop(0, (ROWS + 2 * d) // 2)
        def _(i):
            pair = [padded(rows((2 * i + n) * PITCH, PITCH, 8)) for n in (0, 1)]
            for c in (-1, 0, 1):
                both = [row[8 + c * d : 16 + c * d] for row in pair]
                V[c + 1, rows(i * 16, 16), :] = jnp.concatenate(both, axis=0).astype(BF16)

        if d == 1:

            @pl.loop(0, ROWS // 2)
            def _(i):
                pair = [padded(rows((2 * i + n + 1) * PITCH, PITCH, 8)) for n in (0, 1)]
                for c in (-1, 0, 1):
                    both = [row[8 + c * d : 16 + c * d] for row in pair]
                    U[c + 1, rows(i * 16, 16), :] = jnp.concatenate(both, axis=0).astype(BF16)

    def near_put(d, chunk, values):
        for i in range(8):
            pad_put(rows((d + chunk * 8 + i) * PITCH + 8, 8, 8), values[i * 8 : i * 8 + 8])

    def far_put(chunk, values):
        pad_put(rows(chunk * 128 + 32, 64, 8), values)

    def far_versions(s):
        for c in (-1, 0, 1):
            V[c + 1, pl.ds(0, s * 64), :] = jnp.zeros((s * 64, CH), BF16)
            V[c + 1, pl.ds((8 + s) * 64, s * 64), :] = jnp.zeros((s * 64, CH), BF16)

            @pl.loop(0, 8)
            def _(i, c=c):
                V[c + 1, rows((i + s) * 64, 64), :] = padded(rows(i * 128 + 32 + c * s * 8, 64, 8)).astype(BF16)

    def sources(step, sign):
        found = []
        for r, c in TAPS:
            r, c = sign * r, sign * c
            if step == 8 and r == 0:
                found.append((U.at[c + 1], 0))
            else:
                found.append((V.at[c + 1], (1 + r) * step))
        return found

    BLOCK = 256

    def convolve(k, step, sign, finish):
        found = sources(step, sign)

        @pl.loop(0, CELLS // BLOCK)
        def _(m):
            left = jnp.concatenate(
                [ref[rows(m * BLOCK + start, BLOCK), :] for ref, start in found], axis=1
            )
            if sign == 1:
                result = jnp.dot(left, W[k], preferred_element_type=F32)
            else:
                right = jnp.concatenate([W[k, t * CH : (t + 1) * CH, :] for t in range(9)], axis=1)
                result = lax.dot_general(left, right, (((1,), (1,)), ((), ())), preferred_element_type=F32)
            finish(rows(m * BLOCK, BLOCK), result)

    def act(k, slot, put):
        gain = gains[k : k + 1, :]

        @pl.loop(0, 8)
        def _(chunk):
            unit, _ = normed(S[slot, rows(chunk * 64, 64), :])
            acted = gelu(unit * gain).astype(BF16)
            D[rows(chunk * 64, 64), :] = acted.astype(F32)
            put(chunk, acted.astype(F32))

    def turn(k):
        AT[k] = D[...].T.astype(BF16)

    def kernel_gradient(k, step):
        found = sources(step, -1)
        for first in (0, 2, 4, 6, 8):
            pair = found[first : first + 2]
            right = jnp.concatenate([ref[pl.ds(start, CELLS), :] for ref, start in pair], axis=1)
            both = jnp.dot(AT[k], right, preferred_element_type=F32)
            for n in range(len(pair)):
                G[pl.ds((first + n) * CH, CH), :] = both[:, n * CH : (n + 1) * CH]

    def plane_send(slot):
        @pl.loop(1, 32)
        def _(step):
            q = (me + step) % 32
            pltpu.make_async_remote_copy(
                src_ref=AS.at[slot, rows(q * 16, 16)],
                dst_ref=AL.at[slot, rows(me * 16, 16)],
                send_sem=as_sem.at[slot],
                recv_sem=ar_sem.at[slot],
                device_id=plane(q),
                device_id_type=MESH,
            ).start()

        AL[slot, rows(me * 16, 16), :] = AS[slot, rows(me * 16, 16), :]

    def plane_wait(slot, sem):
        part = AL.at[slot, pl.ds(0, 31 * 16)]
        pltpu.make_async_copy(part, part, sem.at[slot]).wait()

    def to_far(slot, load):
        @pl.loop(0, 32)
        def _(q):
            both = jnp.concatenate([load(rows(q * 8, 8, 8)), load(rows(q * 8 + 256, 8, 8))], axis=0)
            AS[slot, rows(q * 16, 16), :] = both.astype(BF16)

        plane_send(slot)

    def at_far(slot, store):
        plane_wait(slot, ar_sem)

        @pl.loop(0, 32)
        def _(q):
            both = AL[slot, rows(q * 16, 16), :].astype(F32)
            base = ((q // 8) * 16 + q % 8) * 8
            store(rows(base, 8, 8), both[0:8])
            store(rows(base + 64, 8, 8), both[8:16])

    def to_near(slot, load):
        @pl.loop(0, 32)
        def _(q):
            base = ((q // 8) * 16 + q % 8) * 8
            both = jnp.concatenate([load(rows(base, 8, 8)), load(rows(base + 64, 8, 8))], axis=0)
            AS[slot, rows(q * 16, 16), :] = both.astype(BF16)

        plane_send(slot)

    def at_near(slot, store):
        plane_wait(slot, ar_sem)

        @pl.loop(0, 32)
        def _(q):
            both = AL[slot, rows(q * 16, 16), :].astype(F32)
            store(rows(q * 8, 8, 8), both[0:8])
            store(rows(q * 8 + 256, 8, 8), both[8:16])

    def sibling_copy(k, p):
        return pltpu.make_async_remote_copy(
            src_ref=SB.at[k % 2, p, rows((1 - core) * 2048, 2048)],
            dst_ref=R0.at[k, p],
            send_sem=rs_sem.at[k, p, 0],
            recv_sem=rr_sem.at[k, p, 0],
            device_id=(gx + 1 - 2 * core, gy),
            device_id_type=MESH,
        )

    def held(p, level):
        base, size = core * 64, 64
        for n in range(level):
            size = size // 4
            base = base + here[ORDERS[p][n]] * size
        return base, size

    def axis_copy(k, p, level, step):
        axis = ORDERS[p][level - 1]
        base, size = held(p, level - 1)
        size = size // 4
        to = (here[axis] + step) % 4
        land = (None, L1, L2, L3)[level]
        return pltpu.make_async_remote_copy(
            src_ref=SB.at[k % 2, p, rows((base + to * size) * 32, size * 32)],
            dst_ref=land.at[k, p, step - 1],
            send_sem=rs_sem.at[k, p, level * 3 - 3 + step],
            recv_sem=rr_sem.at[k, p, level * 3 - 3 + step],
            device_id=device(core, {**here, axis: to}),
            device_id_type=MESH,
        )

    def reduce_0(k):
        if k < 2:
            reduce_sent(k + 2)

        @pl.loop(0, 16)
        def _(group):
            for n in range(8):
                chunk = group * 8 + n
                at = {"x": n % 4, "z": (chunk // 4) % 4, "y": (chunk // 64) * 2 + (chunk // 16) % 2}
                skip = CHUNK * n % 8
                values = G[rows(group * 8 * CHUNK + CHUNK * n - skip, 40, 8), :][skip : skip + 32]
                for p in range(3):
                    a, b, c = (at[axis] for axis in ORDERS[p])
                    to = ((chunk // 32) % 2) * 64 + a * 16 + b * 4 + c
                    SB[k % 2, p, rows(to * 32, 32), :] = values[:, p * 128 : (p + 1) * 128].astype(BF16)

        for p in range(3):
            sibling_copy(k, p).start()

    def reduce_sent(k):
        for p in range(3):
            sibling_copy(k, p).wait_send()
            for level in (1, 2, 3):
                for step in (1, 2, 3):
                    axis_copy(k, p, level, step).wait_send()

    def reduce_1(k):
        for p in range(3):
            sibling_copy(k, p).wait_recv()

            @pl.loop(0, 8)
            def _(i, p=p):
                own = rows(core * 2048 + i * 256, 256)
                total = SB[k % 2, p, own, :].astype(F32) + R0[k, p, rows(i * 256, 256), :].astype(F32)
                SB[k % 2, p, own, :] = total.astype(BF16)

            for step in (2, 1, 3):
                axis_copy(k, p, 1, step).start()

    def gathered(k, p, level, part, start):
        land = (None, L1, L2, L3)[level]
        base, _ = held(p, level)
        total = SB[k % 2, p, rows(base * 32 + start, part), :].astype(F32)
        for step in (1, 2, 3):
            total = total + land[k, p, step - 1, rows(start, part), :].astype(F32)
        return total

    def reduce_next(k, level):
        for p in range(3):
            for step in (1, 2, 3):
                axis_copy(k, p, level, step).wait_recv()
            base, size = held(p, level)
            part = 128

            @pl.loop(0, size * 32 // part)
            def _(i, p=p, base=base):
                total = gathered(k, p, level, part, i * part)
                SB[k % 2, p, rows(base * 32 + i * part, part), :] = total.astype(BF16)

            for step in (2, 1, 3):
                axis_copy(k, p, level + 1, step).start()

    def reduce_last(k):
        for p in range(3):
            for step in (1, 2, 3):
                axis_copy(k, p, 3, step).wait_recv()
            wg_out[k, :, p * 128 : (p + 1) * 128] = gathered(k, p, 3, 32, 0) * (1.0 / 256.0)

    @pl.loop(0, 8)
    def _(chunk):
        S[0, rows(chunk * 64, 64), :] = x_ref[rows(chunk * 64, 64), :].astype(F32)

    act(0, 0, lambda chunk, values: near_put(1, chunk, values))
    pl.semaphore_wait(barrier, greeted)
    halo_send(0, 1)
    to_far(0, lambda at: cot[at, :])
    turn(0)
    loads[0].wait()
    halo_receive(0, 1)
    near_versions(1)

    def grow(slot):
        def finish(at, result):
            S[slot + 1, at, :] = S[slot, at, :] + result

        return finish

    convolve(0, 8, 1, grow(0))

    act(1, 1, lambda chunk, values: near_put(4, chunk, values))
    halo_send(1, 4)
    turn(1)
    loads[1].wait()
    halo_receive(1, 4)
    near_versions(4)
    convolve(1, 32, 1, grow(1))

    to_far(1, lambda at: S[2, at, :])
    loads[2].wait()
    loads[3].wait()

    @pl.loop(0, 8)
    def _(i):
        pad_put(rows(i * 128, 32, 8), jnp.zeros((32, CH), F32))
        pad_put(rows(i * 128 + 96, 32, 8), jnp.zeros((32, CH), F32))

    def store_stream(at, values):
        S[3, at, :] = values

    at_far(1, store_stream)

    act(2, 3, far_put)
    far_versions(1)
    convolve(2, 64, 1, grow(3))
    turn(2)
    act(3, 4, far_put)
    far_versions(4)

    def keep_updates(at, result):
        S[5, at, :] = (S[4, at, :] - S[3, at, :]) + result

    convolve(3, 256, 1, keep_updates)
    to_near(2, lambda at: S[5, at, :])
    turn(3)

    def store_gradient(at, values):
        S[6, at, :] = values

    at_far(0, store_gradient)

    def put_gradient(slot, put):
        @pl.loop(0, 8)
        def _(chunk):
            put(chunk, S[slot, rows(chunk * 64, 64), :].astype(BF16).astype(F32))

    def keep_d_act(at, result):
        D[at, :] = result

    def pull(k, stream_slot, finish):
        gain = gains[k : k + 1, :]

        @pl.loop(0, 8)
        def _(chunk):
            at = rows(chunk * 64, 64)
            finish(chunk, at, pulled(S[stream_slot, at, :], gain, D[at, :]))

    put_gradient(6, far_put)
    far_versions(4)
    kernel_gradient(3, 256)
    reduce_0(3)
    convolve(3, 256, -1, keep_d_act)

    def far_3(chunk, at, pulled_back):
        S[5, at, :] = pulled_back
        S[6, at, :] = S[6, at, :] + pulled_back

    pull(3, 4, far_3)
    put_gradient(6, far_put)
    far_versions(1)
    reduce_1(3)
    convolve(2, 64, -1, keep_d_act)

    def far_2(chunk, at, pulled_back):
        S[5, at, :] = S[5, at, :] + pulled_back

    pull(2, 3, far_2)
    to_near(3, lambda at: S[5, at, :])
    reduce_next(3, 1)
    kernel_gradient(2, 64)
    reduce_0(2)

    def store_output(at, values):
        out[at, :] = S[2, at, :] + values

    at_near(2, store_output)

    def store_near_gradient(at, values):
        S[6, at, :] = cot[at, :] + values

    at_near(3, store_near_gradient)
    put_gradient(6, lambda chunk, values: near_put(4, chunk, values))
    halo_send(2, 4)
    reduce_next(3, 2)
    reduce_1(2)
    halo_receive(2, 4)
    near_versions(4)
    convolve(1, 32, -1, keep_d_act)

    def near_1(chunk, at, pulled_back):
        total = S[6, at, :] + pulled_back
        S[6, at, :] = total
        near_put(1, chunk, total.astype(BF16).astype(F32))

    pull(1, 1, near_1)
    halo_send(3, 1)
    reduce_last(3)
    reduce_next(2, 1)
    kernel_gradient(1, 32)
    reduce_0(1)
    halo_receive(3, 1)
    near_versions(1)
    kernel_gradient(0, 8)
    reduce_next(2, 2)
    reduce_1(1)
    reduce_last(2)
    reduce_0(0)
    convolve(0, 8, -1, keep_d_act)

    def near_0(chunk, at, pulled_back):
        ig[at, :] = S[6, at, :] + pulled_back

    reduce_next(1, 1)
    pull(0, 0, near_0)
    reduce_1(0)
    reduce_next(1, 2)
    reduce_next(0, 1)
    reduce_last(1)
    reduce_next(0, 2)
    reduce_last(0)

    reduce_sent(1)
    reduce_sent(0)
    for slot in range(4):
        plane_wait(slot, as_sem)
    for slot, d in enumerate((1, 4, 4, 1)):
        for index, direction in enumerate(DIRS):

            @pl.when(exists(direction))
            def _(slot=slot, d=d, index=index):
                halo_copy(slot, d, index).wait_send()


def body(inputs, norm_gains, weights, cotangent):
    vmem = pl.BlockSpec(memory_space=pltpu.VMEM)
    out, input_grad, shares = pl.pallas_call(
        kernel,
        out_shape=(
            jax.ShapeDtypeStruct((CELLS, CH), F32),
            jax.ShapeDtypeStruct((CELLS, CH), F32),
            jax.ShapeDtypeStruct((4, 32, CH), F32),
        ),
        in_specs=[vmem, vmem, pl.BlockSpec(memory_space=pl.ANY), vmem],
        out_specs=(vmem, vmem, vmem),
        scratch_shapes=[
            pltpu.VMEM((4, 9 * CH, CH), BF16),
            pltpu.VMEM((7, CELLS, CH), F32),
            pltpu.VMEM((CELLS, CH), F32),
            pltpu.VMEM((4, CH, CELLS), BF16),
            pltpu.VMEM((3, 72 * PITCH, 128), F32),
            pltpu.VMEM((3, 1024, CH), BF16),
            pltpu.VMEM((3, CELLS, CH), BF16),
            pltpu.VMEM((9 * CH + 16, CH), F32),
            pltpu.VMEM((2, 3, 4096, 128), BF16),
            pltpu.VMEM((4, 3, 2048, 128), BF16),
            pltpu.VMEM((4, 3, 3, 512, 128), BF16),
            pltpu.VMEM((4, 3, 3, 128, 128), BF16),
            pltpu.VMEM((4, 3, 3, 32, 128), BF16),
            pltpu.VMEM((4, CELLS, CH), BF16),
            pltpu.VMEM((4, CELLS, CH), BF16),
            pltpu.VMEM((4, 576, CH), BF16),
            pltpu.VMEM((4, 704, CH), BF16),
            pltpu.SemaphoreType.DMA((4,)),
            pltpu.SemaphoreType.DMA((4, 8)),
            pltpu.SemaphoreType.DMA((4, 8)),
            pltpu.SemaphoreType.DMA((4,)),
            pltpu.SemaphoreType.DMA((4,)),
            pltpu.SemaphoreType.DMA((4, 3, 10)),
            pltpu.SemaphoreType.DMA((4, 3, 10)),
        ],
        compiler_params=pltpu.CompilerParams(
            collective_id=0, has_side_effects=True, vmem_limit_bytes=64 * 1024 * 1024
        ),
        cost_estimate=pl.CostEstimate(flops=16_300_000_000, bytes_accessed=15_000_000, transcendentals=4_000_000),
    )(inputs.reshape(CELLS, CH), norm_gains, weights, cotangent.reshape(CELLS, CH))
    shape = (ROWS, COLS, CH)
    return (
        out.reshape(shape),
        input_grad.reshape(shape),
        shares[:, :CHUNK].reshape(4, CHUNK * CH),
    )


def solution(mesh):
    placed = (P("gx", "gy", None), P(), P(), P("gx", "gy", None))
    return jax.shard_map(
        body,
        mesh=mesh,
        in_specs=placed,
        out_specs=(P("gx", "gy", None), P("gx", "gy", None), P(None, ("gx", "gy"))),
        check_vma=False,
    )
```

```python
import math

import jax
import jax.numpy as jnp
from jax import lax
from jax.experimental import pallas as pl
from jax.experimental.pallas import tpu as pltpu
from jax.sharding import PartitionSpec as P

F32 = jnp.float32
BF16 = jnp.bfloat16
MESH = pl.DeviceIdType.MESH
CH = 384
ROWS, COLS = 64, 8
CELLS = ROWS * COLS
TAPS = tuple((r, c) for r in (-1, 0, 1) for c in (-1, 0, 1))
EPSILON = 1e-05
ROOT = math.sqrt(2.0 / math.pi)
CUBIC = 0.044715
PITCH = 24
DIRS = ((0, -1), (0, 1), (-1, 0), (1, 0), (-1, -1), (-1, 1), (1, -1), (1, 1))
CHUNK = 27
ORDERS = (("x", "y", "z"), ("y", "z", "x"), ("z", "x", "y"))


def aligned(value, step):
    return value if isinstance(value, int) else pl.multiple_of(value, step)


def rows(start, size, step=16):
    return pl.ds(aligned(start, step), size)


def normed(stream):
    average = jnp.mean(stream, axis=-1, keepdims=True)
    centred = stream - average
    spread = jnp.mean(centred * centred, axis=-1, keepdims=True)
    inverse = lax.rsqrt(spread + EPSILON)
    return centred * inverse, inverse


def gelu(u):
    half = 0.5 * u
    return half + half * jnp.tanh(u * (ROOT + (ROOT * CUBIC) * (u * u)))


def gelu_slope(u):
    square = u * u
    t = jnp.tanh(u * (ROOT + (ROOT * CUBIC) * square))
    rest = (1.0 - t) * u * (ROOT + (3.0 * ROOT * CUBIC) * square)
    return (0.5 + 0.5 * t) * (1.0 + rest)


def pulled(unit, inverse, gain, d_act):
    d_unit = d_act * gelu_slope(unit * gain) * gain
    first = jnp.mean(d_unit, axis=-1, keepdims=True)
    second = jnp.mean(d_unit * unit, axis=-1, keepdims=True)
    return inverse * (d_unit - first - unit * second)


def strip_rows(d):
    return (ROWS * d, ROWS * d, max(COLS * d, 16), max(COLS * d, 16))


def kernel(
    x_hbm, gains, w_hbm, cot_hbm, out, ig, wg_out,
    W, X, CT, S, D, UN, IV, AT, F, V, U, G, SB, R0, L1, L2, L3, AS, AL, HS, HL,
    w_sem, io_sem, hs_sem, hr_sem, as_sem, ar_sem, rs_sem, rr_sem,
):
    gx, gy = lax.axis_index("gx"), lax.axis_index("gy")
    core, y = gx & 1, (gx >> 1) * 2 + (gy >> 4)
    z, x = (gy >> 2) & 3, gy & 3
    here = {"x": x, "y": y, "z": z}
    me = gx * 8 + (gy >> 2)

    def device(core_of, at):
        return ((at["y"] >> 1) * 2 + core_of, (at["y"] & 1) * 16 + at["z"] * 4 + at["x"])

    def plane(q):
        return (q >> 3, (q & 7) * 4 + x)

    def exists(direction):
        r, c = gx + direction[0], gy + direction[1]
        return (r >= 0) & (r < 4) & (c >= 0) & (c < 32)

    barrier = pltpu.get_barrier_semaphore()

    def greet(target):
        pl.semaphore_signal(barrier, inc=1, device_id=target, device_id_type=MESH)

    @pl.loop(1, 32)
    def _(step):
        greet(plane((me + step) & 31))

    for step in (1, 2, 3):
        greet(device(core, {**here, "x": (x + step) & 3}))
    greeted = 34
    for direction in DIRS:
        there = exists(direction)

        @pl.when(there)
        def _(direction=direction):
            greet((gx + direction[0], gy + direction[1]))

        greeted = greeted + there.astype(jnp.int32)

    load_x = pltpu.make_async_copy(x_hbm, X, io_sem.at[0])
    load_x.start()
    load_cot = pltpu.make_async_copy(cot_hbm, CT, io_sem.at[1])
    load_cot.start()
    loads = []
    for k in range(4):
        loads.append(pltpu.make_async_copy(w_hbm.at[k], W.at[k], w_sem.at[k]))
        loads[k].start()

    def padded(at):
        return jnp.concatenate([F[p, at, :] for p in range(3)], axis=1)

    def pad_put(at, values):
        for p in range(3):
            F[p, at, :] = values[:, p * 128 : (p + 1) * 128]

    def halo_copy(slot, d, index):
        sizes = strip_rows(d)
        source = (0, 1, 2, 3, 2, 2, 3, 3)[index]
        size = sizes[source]
        starts = [sum(sizes[:i]) for i in range(4)]
        landed = (0, 1, 2, 3, 2, 2, 3, 3)
        lands = [sum(sizes[landed[j]] for j in range(i)) for i in range(8)]
        direction = DIRS[index]
        opposite = DIRS.index((-direction[0], -direction[1]))
        return pltpu.make_async_remote_copy(
            src_ref=HS.at[slot, pl.ds(starts[source], size)],
            dst_ref=HL.at[slot, pl.ds(lands[opposite], size)],
            send_sem=hs_sem.at[slot, index],
            recv_sem=hr_sem.at[slot, opposite],
            device_id=(gx + direction[0], gy + direction[1]),
            device_id_type=MESH,
        )

    def halo_send(slot, d):
        sizes = strip_rows(d)
        at = 0
        for first in (0, COLS - d):
            for j in range(d):
                column = padded(pl.ds(d * PITCH + 8 + first + j, ROWS, stride=PITCH))
                HS[slot, pl.ds(at + j * ROWS, ROWS), :] = column.astype(BF16)
            at += ROWS * d
        count = sizes[2] // COLS
        for first in (0, ROWS - count):
            for i in range(0, count, 2):
                pair = [padded(pl.ds((d + first + i + n) * PITCH + 8, 8)) for n in (0, 1)]
                HS[slot, pl.ds(at + i * 8, 16), :] = jnp.concatenate(pair, axis=0).astype(BF16)
            at += sizes[2]
        for index, direction in enumerate(DIRS):

            @pl.when(exists(direction))
            def _(index=index):
                halo_copy(slot, d, index).start()

    def halo_sent(slot, d):
        for index, direction in enumerate(DIRS):

            @pl.when(exists(direction))
            def _(index=index):
                halo_copy(slot, d, index).wait_send()

    def halo_receive(slot, d):
        sizes = strip_rows(d)
        landed = (0, 1, 2, 3, 2, 2, 3, 3)
        lands = [sum(sizes[landed[j]] for j in range(i)) for i in range(8)]
        count = sizes[2] // COLS
        for index, direction in enumerate(DIRS):
            there = exists(direction)

            def put(values, index=index, direction=direction):
                if direction[0] == 0:
                    first = 8 - d if direction[1] < 0 else 16
                    for j in range(d):
                        pad_put(pl.ds(d * PITCH + first + j, ROWS, stride=PITCH), values(j * ROWS, ROWS))
                else:
                    first = 0 if direction[0] < 0 else d + ROWS
                    skip = count - d if direction[0] < 0 else 0
                    for i in range(0, count, 2):
                        both = values(i * 8, 16)
                        for n in (0, 1):
                            row = i + n - skip
                            if 0 <= row < d:
                                start = (first + row) * PITCH + 8 + 8 * direction[1]
                                pad_put(pl.ds(start, 8), both[n * 8 : n * 8 + 8])

            @pl.when(there)
            def _(index=index, direction=direction, put=put):
                opposite = DIRS.index((-direction[0], -direction[1]))
                halo_copy(slot, d, opposite).wait_recv()
                put(lambda at, size: HL[slot, pl.ds(lands[index] + at, size), :].astype(F32))

            @pl.when(jnp.logical_not(there))
            def _(put=put):
                put(lambda at, size: jnp.zeros((size, CH), F32))

    def near_versions(d):
        @pl.loop(0, (ROWS + 2 * d) // 2)
        def _(i):
            pair = [padded(rows((2 * i + n) * PITCH, PITCH, 8)) for n in (0, 1)]
            for c in (-1, 0, 1):
                both = [row[8 + c * d : 16 + c * d] for row in pair]
                V[c + 1, rows(i * 16, 16), :] = jnp.concatenate(both, axis=0).astype(BF16)

        if d == 1:

            @pl.loop(0, ROWS // 2)
            def _(i):
                pair = [padded(rows((2 * i + n + 1) * PITCH, PITCH, 8)) for n in (0, 1)]
                for c in (-1, 0, 1):
                    both = [row[8 + c * d : 16 + c * d] for row in pair]
                    U[c + 1, rows(i * 16, 16), :] = jnp.concatenate(both, axis=0).astype(BF16)

    def near_put(d, chunk, values):
        for i in range(8):
            pad_put(rows((d + chunk * 8 + i) * PITCH + 8, 8, 8), values[i * 8 : i * 8 + 8])

    def far_put(chunk, values):
        pad_put(rows(chunk * 128 + 32, 64, 8), values)

    def far_versions(s):
        for c in (-1, 0, 1):
            V[c + 1, pl.ds(0, s * 64), :] = jnp.zeros((s * 64, CH), BF16)
            V[c + 1, pl.ds((8 + s) * 64, s * 64), :] = jnp.zeros((s * 64, CH), BF16)

            @pl.loop(0, 8)
            def _(i, c=c):
                V[c + 1, rows((i + s) * 64, 64), :] = padded(rows(i * 128 + 32 + c * s * 8, 64, 8)).astype(BF16)

    def sources(step, sign):
        found = []
        for r, c in TAPS:
            r, c = sign * r, sign * c
            if step == 8 and r == 0:
                found.append((U.at[c + 1], 0))
            else:
                found.append((V.at[c + 1], (1 + r) * step))
        return found

    BLOCK = 256

    def convolve(k, step, sign, finish):
        found = sources(step, sign)

        @pl.loop(0, CELLS // BLOCK)
        def _(m):
            left = jnp.concatenate(
                [ref[rows(m * BLOCK + start, BLOCK), :] for ref, start in found], axis=1
            )
            if sign == 1:
                result = jnp.dot(left, W[k], preferred_element_type=F32)
            else:
                right = jnp.concatenate([W[k, t * CH : (t + 1) * CH, :] for t in range(9)], axis=1)
                result = lax.dot_general(left, right, (((1,), (1,)), ((), ())), preferred_element_type=F32)
            finish(rows(m * BLOCK, BLOCK), result)

    def act(k, slot, put):
        gain = gains[k : k + 1, :]

        @pl.loop(0, 8)
        def _(chunk):
            unit, inverse = normed(S[slot, rows(chunk * 64, 64), :])
            UN[k, rows(chunk * 64, 64), :] = unit
            IV[k, rows(chunk * 64, 64), :] = jnp.broadcast_to(inverse, (64, 128))
            acted = gelu(unit * gain).astype(BF16)
            D[rows(chunk * 64, 64), :] = acted.astype(F32)
            put(chunk, acted.astype(F32))

    def turn(k):
        AT[k] = D[...].T.astype(BF16)

    def kernel_gradient(k, step):
        found = sources(step, -1)
        for first in (0, 2, 4, 6, 8):
            pair = found[first : first + 2]
            right = jnp.concatenate([ref[pl.ds(start, CELLS), :] for ref, start in pair], axis=1)
            both = jnp.dot(AT[k], right, preferred_element_type=F32)
            for n in range(len(pair)):
                for p in range(3):
                    G[p, pl.ds((first + n) * CH, CH), :] = both[:, n * CH + p * 128 : n * CH + (p + 1) * 128]

    def plane_send(slot):
        @pl.loop(1, 32)
        def _(step):
            q = (me + step) & 31
            pltpu.make_async_remote_copy(
                src_ref=AS.at[slot, rows(q * 16, 16)],
                dst_ref=AL.at[slot, rows(me * 16, 16)],
                send_sem=as_sem.at[slot],
                recv_sem=ar_sem.at[slot],
                device_id=plane(q),
                device_id_type=MESH,
            ).start()

        AL[slot, rows(me * 16, 16), :] = AS[slot, rows(me * 16, 16), :]

    def plane_wait(slot, sem):
        part = AL.at[slot, pl.ds(0, 31 * 16)]
        pltpu.make_async_copy(part, part, sem.at[slot]).wait()

    def plane_sent(slot):
        plane_wait(slot, as_sem)

    def to_far(slot, load):
        @pl.loop(0, 32)
        def _(q):
            both = jnp.concatenate([load(rows(q * 8, 8, 8)), load(rows(q * 8 + 256, 8, 8))], axis=0)
            AS[slot, rows(q * 16, 16), :] = both.astype(BF16)

        plane_send(slot)

    def at_far(slot, store):
        plane_wait(slot, ar_sem)

        @pl.loop(0, 32)
        def _(q):
            both = AL[slot, rows(q * 16, 16), :].astype(F32)
            base = ((q >> 3) * 16 + (q & 7)) * 8
            store(rows(base, 8, 8), both[0:8])
            store(rows(base + 64, 8, 8), both[8:16])

    def to_near(slot, load):
        @pl.loop(0, 32)
        def _(q):
            base = ((q >> 3) * 16 + (q & 7)) * 8
            both = jnp.concatenate([load(rows(base, 8, 8)), load(rows(base + 64, 8, 8))], axis=0)
            AS[slot, rows(q * 16, 16), :] = both.astype(BF16)

        plane_send(slot)

    def at_near(slot, store):
        plane_wait(slot, ar_sem)

        @pl.loop(0, 32)
        def _(q):
            both = AL[slot, rows(q * 16, 16), :].astype(F32)
            store(rows(q * 8, 8, 8), both[0:8])
            store(rows(q * 8 + 256, 8, 8), both[8:16])

    def sibling_copy(k, p):
        return pltpu.make_async_remote_copy(
            src_ref=SB.at[k % 2, p, rows((1 - core) * 2048, 2048)],
            dst_ref=R0.at[k, p],
            send_sem=rs_sem.at[k, p, 0],
            recv_sem=rr_sem.at[k, p, 0],
            device_id=(gx + 1 - 2 * core, gy),
            device_id_type=MESH,
        )

    def held(p, level):
        base, size = core * 64, 64
        for n in range(level):
            size = size // 4
            base = base + here[ORDERS[p][n]] * size
        return base, size

    def axis_copy(k, p, level, step):
        axis = ORDERS[p][level - 1]
        base, size = held(p, level - 1)
        size = size // 4
        to = (here[axis] + step) & 3
        land = (None, L1, L2, L3)[level]
        return pltpu.make_async_remote_copy(
            src_ref=SB.at[k % 2, p, rows((base + to * size) * 32, size * 32)],
            dst_ref=land.at[k, p, step - 1],
            send_sem=rs_sem.at[k, p, level * 3 - 3 + step],
            recv_sem=rr_sem.at[k, p, level * 3 - 3 + step],
            device_id=device(core, {**here, axis: to}),
            device_id_type=MESH,
        )

    def reduce_0(k):
        if k < 2:
            reduce_sent(k + 2)

        @pl.loop(0, 2)
        def _(high):
            @pl.loop(0, 2)
            def _(half):
                @pl.loop(0, 2)
                def _(low):
                    @pl.loop(0, 2)
                    def _(pair):
                        first = (high * 4 + half * 2 + low) * 16 + pair * 8
                        for p in range(3):
                            eight = G.at[p, rows(first * CHUNK, 8 * CHUNK + 8, 8)]
                            for n in range(8):
                                at = {"x": n % 4, "z": pair * 2 + n // 4, "y": high * 2 + low}
                                a, b, c = (at[axis] for axis in ORDERS[p])
                                to = half * 64 + a * 16 + b * 4 + c
                                SB[k % 2, p, rows(to * 32, 32), :] = eight[pl.ds(CHUNK * n, 32), :].astype(BF16)

        for p in range(3):
            sibling_copy(k, p).start()

    def reduce_sent(k):
        for p in range(3):
            sibling_copy(k, p).wait_send()
            for level in (1, 2, 3):
                for step in (1, 2, 3):
                    axis_copy(k, p, level, step).wait_send()

    def reduce_1(k):
        for p in range(3):
            sibling_copy(k, p).wait_recv()

            @pl.loop(0, 4)
            def _(i, p=p):
                own = rows(core * 2048 + i * 512, 512)
                SB[k % 2, p, own, :] = SB[k % 2, p, own, :] + R0[k, p, rows(i * 512, 512), :]

            for step in (2, 1, 3):
                axis_copy(k, p, 1, step).start()

    def gathered(k, p, level, part, start):
        land = (None, L1, L2, L3)[level]
        base, _ = held(p, level)
        total = SB[k % 2, p, rows(base * 32 + start, part), :].astype(F32)
        for step in (1, 2, 3):
            total = total + land[k, p, step - 1, rows(start, part), :].astype(F32)
        return total

    def reduce_next(k, level):
        for p in range(3):
            for step in (1, 2, 3):
                axis_copy(k, p, level, step).wait_recv()
            base, size = held(p, level)
            part = min(256, size * 32)

            @pl.loop(0, size * 32 // part)
            def _(i, p=p, base=base):
                total = gathered(k, p, level, part, i * part)
                SB[k % 2, p, rows(base * 32 + i * part, part), :] = total.astype(BF16)

            for step in (2, 1, 3):
                axis_copy(k, p, level + 1, step).start()

    def reduce_last(k):
        for p in range(3):
            for step in (1, 2, 3):
                axis_copy(k, p, 3, step).wait_recv()
            total = gathered(k, p, 3, 32, 0) * (1.0 / 256.0)
            for r in range(CHUNK):
                wg_out[k : k + 1, r * CH + p * 128 : r * CH + (p + 1) * 128] = total[r : r + 1]

    load_x.wait()

    @pl.loop(0, 8)
    def _(chunk):
        S[0, rows(chunk * 64, 64), :] = X[rows(chunk * 64, 64), :].astype(F32)

    act(0, 0, lambda chunk, values: near_put(1, chunk, values))
    pl.semaphore_wait(barrier, greeted)
    halo_send(0, 1)
    load_cot.wait()
    to_far(0, lambda at: CT[at, :])
    turn(0)
    loads[0].wait()
    halo_receive(0, 1)
    near_versions(1)

    def grow(slot):
        def finish(at, result):
            S[slot + 1, at, :] = S[slot, at, :] + result

        return finish

    convolve(0, 8, 1, grow(0))

    act(1, 1, lambda chunk, values: near_put(4, chunk, values))
    halo_send(1, 4)
    turn(1)
    loads[1].wait()
    halo_receive(1, 4)
    near_versions(4)
    convolve(1, 32, 1, grow(1))

    to_far(1, lambda at: S[2, at, :])
    loads[2].wait()
    loads[3].wait()

    @pl.loop(0, 8)
    def _(i):
        pad_put(rows(i * 128, 32, 8), jnp.zeros((32, CH), F32))
        pad_put(rows(i * 128 + 96, 32, 8), jnp.zeros((32, CH), F32))

    def store_stream(at, values):
        S[3, at, :] = values

    at_far(1, store_stream)

    act(2, 3, far_put)
    far_versions(1)
    convolve(2, 64, 1, grow(3))
    turn(2)
    act(3, 4, far_put)
    far_versions(4)

    def keep_updates(at, result):
        S[5, at, :] = (S[4, at, :] - S[3, at, :]) + result

    convolve(3, 256, 1, keep_updates)
    to_near(2, lambda at: S[5, at, :])
    turn(3)

    def store_gradient(at, values):
        S[6, at, :] = values

    at_far(0, store_gradient)

    def put_gradient(slot, put):
        @pl.loop(0, 8)
        def _(chunk):
            put(chunk, S[slot, rows(chunk * 64, 64), :].astype(BF16).astype(F32))

    def keep_d_act(at, result):
        D[at, :] = result

    def pull(k, finish):
        gain = gains[k : k + 1, :]

        @pl.loop(0, 8)
        def _(chunk):
            at = rows(chunk * 64, 64)
            finish(chunk, at, pulled(UN[k, at, :], IV[k, at, :][:, :1], gain, D[at, :]))

    put_gradient(6, far_put)
    far_versions(4)
    kernel_gradient(3, 256)
    reduce_0(3)
    convolve(3, 256, -1, keep_d_act)

    def far_3(chunk, at, pulled_back):
        S[5, at, :] = pulled_back
        S[6, at, :] = S[6, at, :] + pulled_back

    pull(3, far_3)
    put_gradient(6, far_put)
    far_versions(1)
    reduce_1(3)
    convolve(2, 64, -1, keep_d_act)

    def far_2(chunk, at, pulled_back):
        S[5, at, :] = S[5, at, :] + pulled_back

    pull(2, far_2)
    to_near(3, lambda at: S[5, at, :])
    reduce_next(3, 1)
    kernel_gradient(2, 64)
    reduce_0(2)

    def store_output(at, values):
        S[2, at, :] = (S[2, at, :] - S[0, at, :]) + values

    at_near(2, store_output)
    save_out = pltpu.make_async_copy(S.at[2], out, io_sem.at[2])
    save_out.start()

    def store_near_gradient(at, values):
        S[6, at, :] = CT[at, :] + values
        S[5, at, :] = values

    at_near(3, store_near_gradient)
    put_gradient(6, lambda chunk, values: near_put(4, chunk, values))
    halo_send(2, 4)
    reduce_next(3, 2)
    reduce_1(2)
    halo_receive(2, 4)
    near_versions(4)
    convolve(1, 32, -1, keep_d_act)

    def near_1(chunk, at, pulled_back):
        total = S[6, at, :] + pulled_back
        S[5, at, :] = S[5, at, :] + pulled_back
        near_put(1, chunk, total.astype(BF16).astype(F32))

    pull(1, near_1)
    halo_send(3, 1)
    reduce_last(3)
    reduce_next(2, 1)
    kernel_gradient(1, 32)
    reduce_0(1)
    halo_receive(3, 1)
    near_versions(1)
    kernel_gradient(0, 8)
    reduce_next(2, 2)
    reduce_1(1)
    reduce_last(2)
    reduce_0(0)
    convolve(0, 8, -1, keep_d_act)

    def near_0(chunk, at, pulled_back):
        S[5, at, :] = S[5, at, :] + pulled_back

    reduce_next(1, 1)
    pull(0, near_0)
    save_ig = pltpu.make_async_copy(S.at[5], ig, io_sem.at[3])
    save_ig.start()
    reduce_1(0)
    reduce_next(1, 2)
    reduce_next(0, 1)
    reduce_last(1)
    reduce_next(0, 2)
    reduce_last(0)

    save_out.wait()
    save_ig.wait()

    reduce_sent(1)
    reduce_sent(0)
    for slot in range(4):
        plane_sent(slot)
    for slot, d in enumerate((1, 4, 4, 1)):
        halo_sent(slot, d)


def body(inputs, norm_gains, weights, cotangent):
    vmem = pl.BlockSpec(memory_space=pltpu.VMEM)
    hbm = pl.BlockSpec(memory_space=pl.ANY)
    out, input_grad, shares = pl.pallas_call(
        kernel,
        out_shape=(
            jax.ShapeDtypeStruct((CELLS, CH), F32),
            jax.ShapeDtypeStruct((CELLS, CH), F32),
            jax.ShapeDtypeStruct((4, CHUNK * CH), F32),
        ),
        in_specs=[hbm, vmem, hbm, hbm],
        out_specs=(hbm, hbm, vmem),
        scratch_shapes=[
            pltpu.VMEM((4, 9 * CH, CH), BF16),
            pltpu.VMEM((CELLS, CH), BF16),
            pltpu.VMEM((CELLS, CH), F32),
            pltpu.VMEM((7, CELLS, CH), F32),
            pltpu.VMEM((CELLS, CH), F32),
            pltpu.VMEM((4, CELLS, CH), F32),
            pltpu.VMEM((4, CELLS, 128), F32),
            pltpu.VMEM((4, CH, CELLS), BF16),
            pltpu.VMEM((3, 72 * PITCH, 128), F32),
            pltpu.VMEM((3, 1024, CH), BF16),
            pltpu.VMEM((3, CELLS, CH), BF16),
            pltpu.VMEM((3, 9 * CH + 8, 128), F32),
            pltpu.VMEM((2, 3, 4096, 128), BF16),
            pltpu.VMEM((4, 3, 2048, 128), BF16),
            pltpu.VMEM((4, 3, 3, 512, 128), BF16),
            pltpu.VMEM((4, 3, 3, 128, 128), BF16),
            pltpu.VMEM((4, 3, 3, 32, 128), BF16),
            pltpu.VMEM((4, CELLS, CH), BF16),
            pltpu.VMEM((4, CELLS, CH), BF16),
            pltpu.VMEM((4, 576, CH), BF16),
            pltpu.VMEM((4, 704, CH), BF16),
            pltpu.SemaphoreType.DMA((4,)),
            pltpu.SemaphoreType.DMA((4,)),
            pltpu.SemaphoreType.DMA((4, 8)),
            pltpu.SemaphoreType.DMA((4, 8)),
            pltpu.SemaphoreType.DMA((4,)),
            pltpu.SemaphoreType.DMA((4,)),
            pltpu.SemaphoreType.DMA((4, 3, 10)),
            pltpu.SemaphoreType.DMA((4, 3, 10)),
        ],
        compiler_params=pltpu.CompilerParams(
            collective_id=0, has_side_effects=True, vmem_limit_bytes=64 * 1024 * 1024
        ),
        cost_estimate=pl.CostEstimate(flops=16_300_000_000, bytes_accessed=15_000_000, transcendentals=4_000_000),
    )(inputs.reshape(CELLS, CH), norm_gains, weights, cotangent.reshape(CELLS, CH))
    shape = (ROWS, COLS, CH)
    return (
        inputs.astype(F32) + out.reshape(shape),
        cotangent + input_grad.reshape(shape),
        shares,
    )


def solution(mesh):
    placed = (P("gx", "gy", None), P(), P(), P("gx", "gy", None))
    return jax.shard_map(
        body,
        mesh=mesh,
        in_specs=placed,
        out_specs=(P("gx", "gy", None), P("gx", "gy", None), P(None, ("gx", "gy"))),
        check_vma=False,
    )
```

```python
import math

import jax
import jax.numpy as jnp
from jax import lax
from jax.experimental import pallas as pl
from jax.experimental.pallas import tpu as pltpu
from jax.sharding import PartitionSpec as P

F32 = jnp.float32
BF16 = jnp.bfloat16
MESH = pl.DeviceIdType.MESH
CH = 384
ROWS, COLS = 64, 8
CELLS = ROWS * COLS
TAPS = tuple((r, c) for r in (-1, 0, 1) for c in (-1, 0, 1))
EPSILON = 1e-05
ROOT = math.sqrt(2.0 / math.pi)
CUBIC = 0.044715
PITCH = 24
DIRS = ((0, -1), (0, 1), (-1, 0), (1, 0), (-1, -1), (-1, 1), (1, -1), (1, 1))
CHUNK = 27
ORDERS = (("x", "y", "z"), ("y", "z", "x"), ("z", "x", "y"))


def aligned(value, step):
    return value if isinstance(value, int) else pl.multiple_of(value, step)


def rows(start, size, step=16):
    return pl.ds(aligned(start, step), size)


def normed(stream):
    average = jnp.mean(stream, axis=-1, keepdims=True)
    centred = stream - average
    spread = jnp.mean(centred * centred, axis=-1, keepdims=True)
    inverse = lax.rsqrt(spread + EPSILON)
    return centred * inverse, inverse


def gelu(u):
    half = 0.5 * u
    return half + half * jnp.tanh(u * (ROOT + (ROOT * CUBIC) * (u * u)))


def gelu_slope(u):
    square = u * u
    t = jnp.tanh(u * (ROOT + (ROOT * CUBIC) * square))
    rest = (1.0 - t) * u * (ROOT + (3.0 * ROOT * CUBIC) * square)
    return (0.5 + 0.5 * t) * (1.0 + rest)


def pulled(unit, inverse, gain, d_act):
    d_unit = d_act * gelu_slope(unit * gain) * gain
    first = jnp.mean(d_unit, axis=-1, keepdims=True)
    second = jnp.mean(d_unit * unit, axis=-1, keepdims=True)
    return inverse * (d_unit - first - unit * second)


def strip_rows(d):
    return (ROWS * d, ROWS * d, max(COLS * d, 16), max(COLS * d, 16))


def kernel(
    x_hbm, gains, w_hbm, cot_hbm, out, ig, wg_out,
    W, X, CT, S, D, UN, IV, AT, F, V, U, G, SB, R0, L1, L2, L3, AS, AL, HS, HL,
    w_sem, io_sem, hs_sem, hr_sem, as_sem, ar_sem, rs_sem, rr_sem,
):
    gx, gy = lax.axis_index("gx"), lax.axis_index("gy")
    core, y = gx & 1, (gx >> 1) * 2 + (gy >> 4)
    z, x = (gy >> 2) & 3, gy & 3
    here = {"x": x, "y": y, "z": z}
    me = gx * 8 + (gy >> 2)

    def device(core_of, at):
        return ((at["y"] >> 1) * 2 + core_of, (at["y"] & 1) * 16 + at["z"] * 4 + at["x"])

    def plane(q):
        return (q >> 3, (q & 7) * 4 + x)

    def exists(direction):
        r, c = gx + direction[0], gy + direction[1]
        return (r >= 0) & (r < 4) & (c >= 0) & (c < 32)

    barrier = pltpu.get_barrier_semaphore()

    def greet(target):
        pl.semaphore_signal(barrier, inc=1, device_id=target, device_id_type=MESH)

    @pl.loop(1, 32)
    def _(step):
        greet(plane((me + step) & 31))

    for step in (1, 2, 3):
        greet(device(core, {**here, "x": (x + step) & 3}))
    greeted = 34
    for direction in DIRS:
        there = exists(direction)

        @pl.when(there)
        def _(direction=direction):
            greet((gx + direction[0], gy + direction[1]))

        greeted = greeted + there.astype(jnp.int32)

    load_x = pltpu.make_async_copy(x_hbm, X, io_sem.at[0])
    load_x.start()
    load_cot = pltpu.make_async_copy(cot_hbm, CT, io_sem.at[1])
    load_cot.start()
    loads = []
    for k in range(4):
        loads.append(pltpu.make_async_copy(w_hbm.at[k], W.at[k], w_sem.at[k]))
        loads[k].start()

    def padded(at):
        return jnp.concatenate([F[p, at, :] for p in range(3)], axis=1)

    def pad_put(at, values):
        for p in range(3):
            F[p, at, :] = values[:, p * 128 : (p + 1) * 128]

    def halo_copy(slot, d, index):
        sizes = strip_rows(d)
        source = (0, 1, 2, 3, 2, 2, 3, 3)[index]
        size = sizes[source]
        starts = [sum(sizes[:i]) for i in range(4)]
        landed = (0, 1, 2, 3, 2, 2, 3, 3)
        lands = [sum(sizes[landed[j]] for j in range(i)) for i in range(8)]
        direction = DIRS[index]
        opposite = DIRS.index((-direction[0], -direction[1]))
        return pltpu.make_async_remote_copy(
            src_ref=HS.at[slot, pl.ds(starts[source], size)],
            dst_ref=HL.at[slot, pl.ds(lands[opposite], size)],
            send_sem=hs_sem.at[slot, index],
            recv_sem=hr_sem.at[slot, opposite],
            device_id=(gx + direction[0], gy + direction[1]),
            device_id_type=MESH,
        )

    def halo_send(slot, d):
        sizes = strip_rows(d)
        at = 0
        for first in (0, COLS - d):
            for j in range(d):
                column = padded(pl.ds(d * PITCH + 8 + first + j, ROWS, stride=PITCH))
                HS[slot, pl.ds(at + j * ROWS, ROWS), :] = column.astype(BF16)
            at += ROWS * d
        count = sizes[2] // COLS
        for first in (0, ROWS - count):
            for i in range(0, count, 2):
                pair = [padded(pl.ds((d + first + i + n) * PITCH + 8, 8)) for n in (0, 1)]
                HS[slot, pl.ds(at + i * 8, 16), :] = jnp.concatenate(pair, axis=0).astype(BF16)
            at += sizes[2]
        for index, direction in enumerate(DIRS):

            @pl.when(exists(direction))
            def _(index=index):
                halo_copy(slot, d, index).start()

    def halo_sent(slot, d):
        for index, direction in enumerate(DIRS):

            @pl.when(exists(direction))
            def _(index=index):
                halo_copy(slot, d, index).wait_send()

    def halo_receive(slot, d):
        sizes = strip_rows(d)
        landed = (0, 1, 2, 3, 2, 2, 3, 3)
        lands = [sum(sizes[landed[j]] for j in range(i)) for i in range(8)]
        count = sizes[2] // COLS
        for index, direction in enumerate(DIRS):
            there = exists(direction)

            def put(values, index=index, direction=direction):
                if direction[0] == 0:
                    first = 8 - d if direction[1] < 0 else 16
                    for j in range(d):
                        pad_put(pl.ds(d * PITCH + first + j, ROWS, stride=PITCH), values(j * ROWS, ROWS))
                else:
                    first = 0 if direction[0] < 0 else d + ROWS
                    skip = count - d if direction[0] < 0 else 0
                    for i in range(0, count, 2):
                        both = values(i * 8, 16)
                        for n in (0, 1):
                            row = i + n - skip
                            if 0 <= row < d:
                                start = (first + row) * PITCH + 8 + 8 * direction[1]
                                pad_put(pl.ds(start, 8), both[n * 8 : n * 8 + 8])

            @pl.when(there)
            def _(index=index, direction=direction, put=put):
                opposite = DIRS.index((-direction[0], -direction[1]))
                halo_copy(slot, d, opposite).wait_recv()
                put(lambda at, size: HL[slot, pl.ds(lands[index] + at, size), :].astype(F32))

            @pl.when(jnp.logical_not(there))
            def _(put=put):
                put(lambda at, size: jnp.zeros((size, CH), F32))

    def near_versions(d):
        @pl.loop(0, (ROWS + 2 * d) // 2)
        def _(i):
            pair = [padded(rows((2 * i + n) * PITCH, PITCH, 8)) for n in (0, 1)]
            for c in (-1, 0, 1):
                both = [row[8 + c * d : 16 + c * d] for row in pair]
                V[c + 1, rows(i * 16, 16), :] = jnp.concatenate(both, axis=0).astype(BF16)

        if d == 1:

            @pl.loop(0, ROWS // 2)
            def _(i):
                pair = [padded(rows((2 * i + n + 1) * PITCH, PITCH, 8)) for n in (0, 1)]
                for c in (-1, 0, 1):
                    both = [row[8 + c * d : 16 + c * d] for row in pair]
                    U[c + 1, rows(i * 16, 16), :] = jnp.concatenate(both, axis=0).astype(BF16)

    def near_put(d, chunk, values):
        for i in range(8):
            pad_put(rows((d + chunk * 8 + i) * PITCH + 8, 8, 8), values[i * 8 : i * 8 + 8])

    def far_put(chunk, values):
        pad_put(rows(chunk * 128 + 32, 64, 8), values)

    def far_versions(s):
        for c in (-1, 0, 1):
            V[c + 1, pl.ds(0, s * 64), :] = jnp.zeros((s * 64, CH), BF16)
            V[c + 1, pl.ds((8 + s) * 64, s * 64), :] = jnp.zeros((s * 64, CH), BF16)

            @pl.loop(0, 8)
            def _(i, c=c):
                V[c + 1, rows((i + s) * 64, 64), :] = padded(rows(i * 128 + 32 + c * s * 8, 64, 8)).astype(BF16)

    def sources(step, sign):
        found = []
        for r, c in TAPS:
            r, c = sign * r, sign * c
            if step == 8 and r == 0:
                found.append((U.at[c + 1], 0))
            else:
                found.append((V.at[c + 1], (1 + r) * step))
        return found

    BLOCK = 256

    def convolve(k, step, sign, finish):
        found = sources(step, sign)

        @pl.loop(0, CELLS // BLOCK)
        def _(m):
            left = jnp.concatenate(
                [ref[rows(m * BLOCK + start, BLOCK), :] for ref, start in found], axis=1
            )
            if sign == 1:
                result = jnp.dot(left, W[k], preferred_element_type=F32)
            else:
                right = jnp.concatenate([W[k, t * CH : (t + 1) * CH, :] for t in range(9)], axis=1)
                result = lax.dot_general(left, right, (((1,), (1,)), ((), ())), preferred_element_type=F32)
            finish(rows(m * BLOCK, BLOCK), result)

    def act(k, slot, put):
        gain = gains[k : k + 1, :]

        @pl.loop(0, 8)
        def _(chunk):
            unit, inverse = normed(S[slot, rows(chunk * 64, 64), :])
            UN[k, rows(chunk * 64, 64), :] = unit
            IV[k, rows(chunk * 64, 64), :] = jnp.broadcast_to(inverse, (64, 128))
            acted = gelu(unit * gain).astype(BF16)
            D[rows(chunk * 64, 64), :] = acted.astype(F32)
            put(chunk, acted.astype(F32))

    def turn(k):
        AT[k] = D[...].T.astype(BF16)

    def kernel_gradient(k, step):
        found = sources(step, -1)
        for first in (0, 2, 4, 6, 8):
            pair = found[first : first + 2]
            right = jnp.concatenate([ref[pl.ds(start, CELLS), :] for ref, start in pair], axis=1)
            both = jnp.dot(AT[k], right, preferred_element_type=F32)
            for n in range(len(pair)):
                for p in range(3):
                    G[p, pl.ds((first + n) * CH, CH), :] = both[:, n * CH + p * 128 : n * CH + (p + 1) * 128]

    def plane_send(slot):
        @pl.loop(1, 32)
        def _(step):
            q = (me + step) & 31
            pltpu.make_async_remote_copy(
                src_ref=AS.at[slot, rows(q * 16, 16)],
                dst_ref=AL.at[slot, rows(me * 16, 16)],
                send_sem=as_sem.at[slot],
                recv_sem=ar_sem.at[slot],
                device_id=plane(q),
                device_id_type=MESH,
            ).start()

        AL[slot, rows(me * 16, 16), :] = AS[slot, rows(me * 16, 16), :]

    def plane_wait(slot, sem):
        part = AL.at[slot, pl.ds(0, 31 * 16)]
        pltpu.make_async_copy(part, part, sem.at[slot]).wait()

    def plane_sent(slot):
        plane_wait(slot, as_sem)

    def to_far(slot, load, now=True):
        @pl.loop(0, 32)
        def _(q):
            both = jnp.concatenate([load(rows(q * 8, 8, 8)), load(rows(q * 8 + 256, 8, 8))], axis=0)
            AS[slot, rows(q * 16, 16), :] = both.astype(BF16)

        if now:
            plane_send(slot)

    def at_far(slot, store):
        plane_wait(slot, ar_sem)

        @pl.loop(0, 32)
        def _(q):
            both = AL[slot, rows(q * 16, 16), :].astype(F32)
            base = ((q >> 3) * 16 + (q & 7)) * 8
            store(rows(base, 8, 8), both[0:8])
            store(rows(base + 64, 8, 8), both[8:16])

    def to_near(slot, load):
        @pl.loop(0, 32)
        def _(q):
            base = ((q >> 3) * 16 + (q & 7)) * 8
            both = jnp.concatenate([load(rows(base, 8, 8)), load(rows(base + 64, 8, 8))], axis=0)
            AS[slot, rows(q * 16, 16), :] = both.astype(BF16)

        plane_send(slot)

    def at_near(slot, store):
        plane_wait(slot, ar_sem)

        @pl.loop(0, 32)
        def _(q):
            both = AL[slot, rows(q * 16, 16), :].astype(F32)
            store(rows(q * 8, 8, 8), both[0:8])
            store(rows(q * 8 + 256, 8, 8), both[8:16])

    def sibling_copy(k, p):
        return pltpu.make_async_remote_copy(
            src_ref=SB.at[k % 3, p, rows((1 - core) * 2048, 2048)],
            dst_ref=R0.at[k, p],
            send_sem=rs_sem.at[k, p, 0],
            recv_sem=rr_sem.at[k, p, 0],
            device_id=(gx + 1 - 2 * core, gy),
            device_id_type=MESH,
        )

    def held(p, level):
        base, size = core * 64, 64
        for n in range(level):
            size = size // 4
            base = base + here[ORDERS[p][n]] * size
        return base, size

    def axis_copy(k, p, level, step):
        axis = ORDERS[p][level - 1]
        base, size = held(p, level - 1)
        size = size // 4
        to = (here[axis] + step) & 3
        land = (None, None, L2, L3)[level]
        return pltpu.make_async_remote_copy(
            src_ref=SB.at[k % 3, p, rows((base + to * size) * 32, size * 32)],
            dst_ref=land.at[k, p, step - 1],
            send_sem=rs_sem.at[k, p, level * 3 + step],
            recv_sem=rr_sem.at[k, p, level * 3 + step],
            device_id=device(core, {**here, axis: to}),
            device_id_type=MESH,
        )

    HOPS = ((2, 0, 1), (2, 1, 3), (1, 1, 1), (3, 0, 3), (1, 0, 1), (3, 1, 3))

    def ring_copy(k, p, slot):
        axis = ORDERS[p][0]
        of, half, by = HOPS[slot]
        start = core * 2048 + ((here[axis] + of) & 3) * 512 + half * 256
        return pltpu.make_async_remote_copy(
            src_ref=SB.at[k % 3, p, rows(start, 256)],
            dst_ref=L1.at[k, p, slot],
            send_sem=rs_sem.at[k, p, 1 + slot],
            recv_sem=rr_sem.at[k, p, 1 + slot],
            device_id=device(core, {**here, axis: (here[axis] + by) & 3}),
            device_id_type=MESH,
        )

    def reduce_0(k):
        if k == 0:
            reduce_sent(3)

        @pl.loop(0, 2)
        def _(high):
            @pl.loop(0, 2)
            def _(half):
                @pl.loop(0, 2)
                def _(low):
                    @pl.loop(0, 2)
                    def _(pair):
                        first = (high * 4 + half * 2 + low) * 16 + pair * 8
                        for p in range(3):
                            eight = G.at[p, rows(first * CHUNK, 8 * CHUNK + 8, 8)]
                            for n in range(8):
                                at = {"x": n % 4, "z": pair * 2 + n // 4, "y": high * 2 + low}
                                a, b, c = (at[axis] for axis in ORDERS[p])
                                to = half * 64 + a * 16 + b * 4 + c
                                SB[k % 3, p, rows(to * 32, 32), :] = eight[pl.ds(CHUNK * n, 32), :].astype(BF16)

        for p in range(3):
            sibling_copy(k, p).start()

    def reduce_sent(k):
        for p in range(3):
            sibling_copy(k, p).wait_send()
            for slot in range(6):
                ring_copy(k, p, slot).wait_send()
            for level in (2, 3):
                for step in (1, 2, 3):
                    axis_copy(k, p, level, step).wait_send()

    def reduce_1(k):
        for p in range(3):
            sibling_copy(k, p).wait_recv()

            @pl.loop(0, 4)
            def _(i, p=p):
                own = rows(core * 2048 + i * 512, 512)
                SB[k % 3, p, own, :] = SB[k % 3, p, own, :] + R0[k, p, rows(i * 512, 512), :]

            for slot in range(4):
                ring_copy(k, p, slot).start()

    def reduce_via(k):
        for p in range(3):
            for slot in (0, 1):
                ring_copy(k, p, slot).wait_recv()
                of, half, _ = HOPS[4 + slot]
                own = rows(core * 2048 + ((here[ORDERS[p][0]] + of) & 3) * 512 + half * 256, 256)
                SB[k % 3, p, own, :] = SB[k % 3, p, own, :] + L1[k, p, slot]
                ring_copy(k, p, 4 + slot).start()

    def gathered(k, p, level, part, start):
        land = (None, None, L2, L3)[level]
        base, _ = held(p, level)
        total = SB[k % 3, p, rows(base * 32 + start, part), :].astype(F32)
        for step in (1, 2, 3):
            total = total + land[k, p, step - 1, rows(start, part), :].astype(F32)
        return total

    def reduce_next(k, level):
        for p in range(3):
            base, size = held(p, level)
            if level == 1:
                for slot in (2, 3, 4, 5):
                    ring_copy(k, p, slot).wait_recv()
                for half, arrived in ((0, (3, 4)), (1, (2, 5))):
                    own = rows(base * 32 + half * 256, 256)
                    total = SB[k % 3, p, own, :].astype(F32)
                    for slot in arrived:
                        total = total + L1[k, p, slot].astype(F32)
                    SB[k % 3, p, own, :] = total.astype(BF16)
            else:
                for step in (1, 2, 3):
                    axis_copy(k, p, level, step).wait_recv()
                total = gathered(k, p, level, size * 32, 0)
                SB[k % 3, p, rows(base * 32, size * 32), :] = total.astype(BF16)

            for step in (2, 1, 3):
                axis_copy(k, p, level + 1, step).start()

    def reduce_last(k):
        for p in range(3):
            for step in (1, 2, 3):
                axis_copy(k, p, 3, step).wait_recv()
            total = gathered(k, p, 3, 32, 0) * (1.0 / 256.0)
            for r in range(CHUNK):
                wg_out[k : k + 1, r * CH + p * 128 : r * CH + (p + 1) * 128] = total[r : r + 1]

    load_x.wait()

    @pl.loop(0, 8)
    def _(chunk):
        S[0, rows(chunk * 64, 64), :] = X[rows(chunk * 64, 64), :].astype(F32)

    act(0, 0, lambda chunk, values: near_put(1, chunk, values))
    pl.semaphore_wait(barrier, greeted)
    halo_send(0, 1)
    load_cot.wait()
    to_far(0, lambda at: CT[at, :], now=False)
    turn(0)
    loads[0].wait()
    halo_receive(0, 1)
    near_versions(1)

    def grow(slot):
        def finish(at, result):
            S[slot + 1, at, :] = S[slot, at, :] + result

        return finish

    convolve(0, 8, 1, grow(0))

    act(1, 1, lambda chunk, values: near_put(4, chunk, values))
    halo_send(1, 4)
    turn(1)
    loads[1].wait()
    halo_receive(1, 4)
    near_versions(4)
    convolve(1, 32, 1, grow(1))

    to_far(1, lambda at: S[2, at, :])
    loads[2].wait()
    loads[3].wait()

    @pl.loop(0, 8)
    def _(i):
        pad_put(rows(i * 128, 32, 8), jnp.zeros((32, CH), F32))
        pad_put(rows(i * 128 + 96, 32, 8), jnp.zeros((32, CH), F32))

    def store_stream(at, values):
        S[3, at, :] = values

    at_far(1, store_stream)
    plane_send(0)

    act(2, 3, far_put)
    far_versions(1)
    convolve(2, 64, 1, grow(3))
    turn(2)
    act(3, 4, far_put)
    far_versions(4)

    def keep_updates(at, result):
        S[5, at, :] = (S[4, at, :] - S[3, at, :]) + result

    convolve(3, 256, 1, keep_updates)
    to_near(2, lambda at: S[5, at, :])
    turn(3)

    def store_gradient(at, values):
        S[6, at, :] = values

    at_far(0, store_gradient)

    def put_gradient(slot, put):
        @pl.loop(0, 8)
        def _(chunk):
            put(chunk, S[slot, rows(chunk * 64, 64), :].astype(BF16).astype(F32))

    def keep_d_act(at, result):
        D[at, :] = result

    def pull(k, finish):
        gain = gains[k : k + 1, :]

        @pl.loop(0, 8)
        def _(chunk):
            at = rows(chunk * 64, 64)
            finish(chunk, at, pulled(UN[k, at, :], IV[k, at, :][:, :1], gain, D[at, :]))

    put_gradient(6, far_put)
    far_versions(4)
    kernel_gradient(3, 256)
    reduce_0(3)
    convolve(3, 256, -1, keep_d_act)

    def far_3(chunk, at, pulled_back):
        S[5, at, :] = pulled_back
        S[6, at, :] = S[6, at, :] + pulled_back

    pull(3, far_3)
    reduce_1(3)
    put_gradient(6, far_put)
    far_versions(1)
    convolve(2, 64, -1, keep_d_act)

    def far_2(chunk, at, pulled_back):
        S[5, at, :] = S[5, at, :] + pulled_back

    pull(2, far_2)
    to_near(3, lambda at: S[5, at, :])
    reduce_via(3)
    kernel_gradient(2, 64)
    reduce_0(2)

    def store_output(at, values):
        S[2, at, :] = (S[2, at, :] - S[0, at, :]) + values

    at_near(2, store_output)
    save_out = pltpu.make_async_copy(S.at[2], out, io_sem.at[2])
    save_out.start()

    def store_near_gradient(at, values):
        S[6, at, :] = CT[at, :] + values
        S[5, at, :] = values

    at_near(3, store_near_gradient)
    put_gradient(6, lambda chunk, values: near_put(4, chunk, values))
    halo_send(2, 4)
    reduce_next(3, 1)
    halo_receive(2, 4)
    near_versions(4)
    reduce_1(2)
    convolve(1, 32, -1, keep_d_act)

    def near_1(chunk, at, pulled_back):
        total = S[6, at, :] + pulled_back
        S[5, at, :] = S[5, at, :] + pulled_back
        near_put(1, chunk, total.astype(BF16).astype(F32))

    pull(1, near_1)
    halo_send(3, 1)
    reduce_next(3, 2)
    reduce_via(2)
    kernel_gradient(1, 32)
    reduce_0(1)
    reduce_next(2, 1)
    halo_receive(3, 1)
    near_versions(1)
    kernel_gradient(0, 8)
    reduce_1(1)
    reduce_last(3)
    reduce_0(0)
    convolve(0, 8, -1, keep_d_act)

    def near_0(chunk, at, pulled_back):
        S[5, at, :] = S[5, at, :] + pulled_back

    reduce_via(1)
    reduce_next(2, 2)
    reduce_1(0)
    pull(0, near_0)
    save_ig = pltpu.make_async_copy(S.at[5], ig, io_sem.at[3])
    save_ig.start()
    reduce_next(1, 1)
    reduce_via(0)
    reduce_last(2)
    reduce_next(1, 2)
    reduce_next(0, 1)
    reduce_last(1)
    reduce_next(0, 2)
    reduce_last(0)

    save_out.wait()
    save_ig.wait()

    for k in (2, 1, 0):
        reduce_sent(k)
    for slot in range(4):
        plane_sent(slot)
    for slot, d in enumerate((1, 4, 4, 1)):
        halo_sent(slot, d)


def body(inputs, norm_gains, weights, cotangent):
    vmem = pl.BlockSpec(memory_space=pltpu.VMEM)
    hbm = pl.BlockSpec(memory_space=pl.ANY)
    out, input_grad, shares = pl.pallas_call(
        kernel,
        out_shape=(
            jax.ShapeDtypeStruct((CELLS, CH), F32),
            jax.ShapeDtypeStruct((CELLS, CH), F32),
            jax.ShapeDtypeStruct((4, CHUNK * CH), F32),
        ),
        in_specs=[hbm, vmem, hbm, hbm],
        out_specs=(hbm, hbm, vmem),
        scratch_shapes=[
            pltpu.VMEM((4, 9 * CH, CH), BF16),
            pltpu.VMEM((CELLS, CH), BF16),
            pltpu.VMEM((CELLS, CH), F32),
            pltpu.VMEM((7, CELLS, CH), F32),
            pltpu.VMEM((CELLS, CH), F32),
            pltpu.VMEM((4, CELLS, CH), F32),
            pltpu.VMEM((4, CELLS, 128), F32),
            pltpu.VMEM((4, CH, CELLS), BF16),
            pltpu.VMEM((3, 72 * PITCH, 128), F32),
            pltpu.VMEM((3, 1024, CH), BF16),
            pltpu.VMEM((3, CELLS, CH), BF16),
            pltpu.VMEM((3, 9 * CH + 8, 128), F32),
            pltpu.VMEM((3, 3, 4096, 128), BF16),
            pltpu.VMEM((4, 3, 2048, 128), BF16),
            pltpu.VMEM((4, 3, 6, 256, 128), BF16),
            pltpu.VMEM((4, 3, 3, 128, 128), BF16),
            pltpu.VMEM((4, 3, 3, 32, 128), BF16),
            pltpu.VMEM((4, CELLS, CH), BF16),
            pltpu.VMEM((4, CELLS, CH), BF16),
            pltpu.VMEM((4, 576, CH), BF16),
            pltpu.VMEM((4, 704, CH), BF16),
            pltpu.SemaphoreType.DMA((4,)),
            pltpu.SemaphoreType.DMA((4,)),
            pltpu.SemaphoreType.DMA((4, 8)),
            pltpu.SemaphoreType.DMA((4, 8)),
            pltpu.SemaphoreType.DMA((4,)),
            pltpu.SemaphoreType.DMA((4,)),
            pltpu.SemaphoreType.DMA((4, 3, 13)),
            pltpu.SemaphoreType.DMA((4, 3, 13)),
        ],
        compiler_params=pltpu.CompilerParams(
            collective_id=0, has_side_effects=True, vmem_limit_bytes=64 * 1024 * 1024
        ),
        cost_estimate=pl.CostEstimate(flops=16_300_000_000, bytes_accessed=15_000_000, transcendentals=4_000_000),
    )(inputs.reshape(CELLS, CH), norm_gains, weights, cotangent.reshape(CELLS, CH))
    shape = (ROWS, COLS, CH)
    return (
        inputs.astype(F32) + out.reshape(shape),
        cotangent + input_grad.reshape(shape),
        shares,
    )


def solution(mesh):
    placed = (P("gx", "gy", None), P(), P(), P("gx", "gy", None))
    return jax.shard_map(
        body,
        mesh=mesh,
        in_specs=placed,
        out_specs=(P("gx", "gy", None), P("gx", "gy", None), P(None, ("gx", "gy"))),
        check_vma=False,
    )
```

```python
import math

import jax
import jax.numpy as jnp
from jax import lax
from jax.experimental import pallas as pl
from jax.experimental.pallas import tpu as pltpu
from jax.sharding import PartitionSpec as P

F32 = jnp.float32
BF16 = jnp.bfloat16
MESH = pl.DeviceIdType.MESH
CH = 384
ROWS, COLS = 64, 8
CELLS = ROWS * COLS
TAPS = tuple((r, c) for r in (-1, 0, 1) for c in (-1, 0, 1))
EPSILON = 1e-05
ROOT = math.sqrt(2.0 / math.pi)
CUBIC = 0.044715
PITCH = 24
DIRS = ((0, -1), (0, 1), (-1, 0), (1, 0), (-1, -1), (-1, 1), (1, -1), (1, 1))
CHUNK = 27
ORDERS = (("x", "y", "z"), ("y", "z", "x"), ("z", "x", "y"))


def aligned(value, step):
    return value if isinstance(value, int) else pl.multiple_of(value, step)


def rows(start, size, step=16):
    return pl.ds(aligned(start, step), size)


def normed(stream):
    average = jnp.mean(stream, axis=-1, keepdims=True)
    centred = stream - average
    spread = jnp.mean(centred * centred, axis=-1, keepdims=True)
    inverse = lax.rsqrt(spread + EPSILON)
    return centred * inverse, inverse


def gelu(u):
    half = 0.5 * u
    return half + half * jnp.tanh(u * (ROOT + (ROOT * CUBIC) * (u * u)))


def gelu_slope(u):
    square = u * u
    t = jnp.tanh(u * (ROOT + (ROOT * CUBIC) * square))
    rest = (1.0 - t) * u * (ROOT + (3.0 * ROOT * CUBIC) * square)
    return (0.5 + 0.5 * t) * (1.0 + rest)


def pulled(unit, inverse, gain, d_act):
    d_unit = d_act * gelu_slope(unit * gain) * gain
    first = jnp.mean(d_unit, axis=-1, keepdims=True)
    second = jnp.mean(d_unit * unit, axis=-1, keepdims=True)
    return inverse * (d_unit - first - unit * second)


def strip_rows(d):
    return (ROWS * d, ROWS * d, max(COLS * d, 16), max(COLS * d, 16))


def kernel(
    x_hbm, gains, w_hbm, cot_hbm, out, ig, wg_out,
    W, X, CT, S, D, UN, IV, AT, F, V, U, G, SB, TB, R0, L1, L2, L3, AS, AL, HS, HL,
    w_sem, io_sem, hs_sem, hr_sem, as_sem, ar_sem, rs_sem, rr_sem,
):
    gx, gy = lax.axis_index("gx"), lax.axis_index("gy")
    core, y = gx & 1, (gx >> 1) * 2 + (gy >> 4)
    z, x = (gy >> 2) & 3, gy & 3
    here = {"x": x, "y": y, "z": z}
    me = gx * 8 + (gy >> 2)

    def device(core_of, at):
        return ((at["y"] >> 1) * 2 + core_of, (at["y"] & 1) * 16 + at["z"] * 4 + at["x"])

    def plane(q):
        return (q >> 3, (q & 7) * 4 + x)

    def exists(direction):
        r, c = gx + direction[0], gy + direction[1]
        return (r >= 0) & (r < 4) & (c >= 0) & (c < 32)

    barrier = pltpu.get_barrier_semaphore()

    def greet(target):
        pl.semaphore_signal(barrier, inc=1, device_id=target, device_id_type=MESH)

    @pl.loop(1, 32)
    def _(step):
        greet(plane((me + step) & 31))

    for step in (1, 2, 3):
        greet(device(core, {**here, "x": (x + step) & 3}))
    greeted = 34
    for direction in DIRS:
        there = exists(direction)

        @pl.when(there)
        def _(direction=direction):
            greet((gx + direction[0], gy + direction[1]))

        greeted = greeted + there.astype(jnp.int32)

    load_x = pltpu.make_async_copy(x_hbm, X, io_sem.at[0])
    load_x.start()
    load_cot = pltpu.make_async_copy(cot_hbm, CT, io_sem.at[1])
    load_cot.start()
    loads = []
    for k in range(4):
        loads.append(pltpu.make_async_copy(w_hbm.at[k], W.at[k], w_sem.at[k]))
        loads[k].start()

    def padded(at):
        return jnp.concatenate([F[p, at, :] for p in range(3)], axis=1)

    def pad_put(at, values):
        for p in range(3):
            F[p, at, :] = values[:, p * 128 : (p + 1) * 128]

    def halo_copy(slot, d, index):
        sizes = strip_rows(d)
        source = (0, 1, 2, 3, 2, 2, 3, 3)[index]
        size = sizes[source]
        starts = [sum(sizes[:i]) for i in range(4)]
        landed = (0, 1, 2, 3, 2, 2, 3, 3)
        lands = [sum(sizes[landed[j]] for j in range(i)) for i in range(8)]
        direction = DIRS[index]
        opposite = DIRS.index((-direction[0], -direction[1]))
        return pltpu.make_async_remote_copy(
            src_ref=HS.at[slot, pl.ds(starts[source], size)],
            dst_ref=HL.at[slot, pl.ds(lands[opposite], size)],
            send_sem=hs_sem.at[slot, index],
            recv_sem=hr_sem.at[slot, opposite],
            device_id=(gx + direction[0], gy + direction[1]),
            device_id_type=MESH,
        )

    def halo_send(slot, d):
        sizes = strip_rows(d)
        at = 0
        for first in (0, COLS - d):
            for j in range(d):
                column = padded(pl.ds(d * PITCH + 8 + first + j, ROWS, stride=PITCH))
                HS[slot, pl.ds(at + j * ROWS, ROWS), :] = column.astype(BF16)
            at += ROWS * d
        count = sizes[2] // COLS
        for first in (0, ROWS - count):
            for i in range(0, count, 2):
                pair = [padded(pl.ds((d + first + i + n) * PITCH + 8, 8)) for n in (0, 1)]
                HS[slot, pl.ds(at + i * 8, 16), :] = jnp.concatenate(pair, axis=0).astype(BF16)
            at += sizes[2]
        for index, direction in enumerate(DIRS):

            @pl.when(exists(direction))
            def _(index=index):
                halo_copy(slot, d, index).start()

    def halo_sent(slot, d):
        for index, direction in enumerate(DIRS):

            @pl.when(exists(direction))
            def _(index=index):
                halo_copy(slot, d, index).wait_send()

    def halo_receive(slot, d):
        sizes = strip_rows(d)
        landed = (0, 1, 2, 3, 2, 2, 3, 3)
        lands = [sum(sizes[landed[j]] for j in range(i)) for i in range(8)]
        count = sizes[2] // COLS
        for index, direction in enumerate(DIRS):
            there = exists(direction)

            def put(values, index=index, direction=direction):
                if direction[0] == 0:
                    first = 8 - d if direction[1] < 0 else 16
                    for j in range(d):
                        pad_put(pl.ds(d * PITCH + first + j, ROWS, stride=PITCH), values(j * ROWS, ROWS))
                else:
                    first = 0 if direction[0] < 0 else d + ROWS
                    skip = count - d if direction[0] < 0 else 0
                    for i in range(0, count, 2):
                        both = values(i * 8, 16)
                        for n in (0, 1):
                            row = i + n - skip
                            if 0 <= row < d:
                                start = (first + row) * PITCH + 8 + 8 * direction[1]
                                pad_put(pl.ds(start, 8), both[n * 8 : n * 8 + 8])

            @pl.when(there)
            def _(index=index, direction=direction, put=put):
                opposite = DIRS.index((-direction[0], -direction[1]))
                halo_copy(slot, d, opposite).wait_recv()
                put(lambda at, size: HL[slot, pl.ds(lands[index] + at, size), :].astype(F32))

            @pl.when(jnp.logical_not(there))
            def _(put=put):
                put(lambda at, size: jnp.zeros((size, CH), F32))

    def near_versions(d):
        @pl.loop(0, (ROWS + 2 * d) // 2, unroll=3 if d == 1 else 4)
        def _(i):
            pair = [padded(rows((2 * i + n) * PITCH, PITCH, 8)) for n in (0, 1)]
            for c in (-1, 0, 1):
                both = [row[8 + c * d : 16 + c * d] for row in pair]
                V[c + 1, rows(i * 16, 16), :] = jnp.concatenate(both, axis=0).astype(BF16)

        if d == 1:

            @pl.loop(0, ROWS // 2, unroll=4)
            def _(i):
                pair = [padded(rows((2 * i + n + 1) * PITCH, PITCH, 8)) for n in (0, 1)]
                for c in (-1, 0, 1):
                    both = [row[8 + c * d : 16 + c * d] for row in pair]
                    U[c + 1, rows(i * 16, 16), :] = jnp.concatenate(both, axis=0).astype(BF16)

    def near_put(d, chunk, values):
        for i in range(8):
            pad_put(rows((d + chunk * 8 + i) * PITCH + 8, 8, 8), values[i * 8 : i * 8 + 8])

    def far_put(chunk, values):
        pad_put(rows(chunk * 128 + 32, 64, 8), values)

    def far_versions(s):
        for c in (-1, 0, 1):
            V[c + 1, pl.ds(0, s * 64), :] = jnp.zeros((s * 64, CH), BF16)
            V[c + 1, pl.ds((8 + s) * 64, s * 64), :] = jnp.zeros((s * 64, CH), BF16)

            @pl.loop(0, 8, unroll=4)
            def _(i, c=c):
                V[c + 1, rows((i + s) * 64, 64), :] = padded(rows(i * 128 + 32 + c * s * 8, 64, 8)).astype(BF16)

    def sources(step, sign):
        found = []
        for r, c in TAPS:
            r, c = sign * r, sign * c
            if step == 8 and r == 0:
                found.append((U.at[c + 1], 0))
            else:
                found.append((V.at[c + 1], (1 + r) * step))
        return found

    BLOCK = 256

    def convolve(k, step, sign, finish):
        found = sources(step, sign)

        @pl.loop(0, CELLS // BLOCK)
        def _(m):
            left = jnp.concatenate(
                [ref[rows(m * BLOCK + start, BLOCK), :] for ref, start in found], axis=1
            )
            if sign == 1:
                result = jnp.dot(left, W[k], preferred_element_type=F32)
            else:
                right = jnp.concatenate([W[k, t * CH : (t + 1) * CH, :] for t in range(9)], axis=1)
                result = lax.dot_general(left, right, (((1,), (1,)), ((), ())), preferred_element_type=F32)
            finish(rows(m * BLOCK, BLOCK), result)

    def act(k, slot, put):
        gain = gains[k : k + 1, :]

        @pl.loop(0, 8, unroll=4)
        def _(chunk):
            unit, inverse = normed(S[slot, rows(chunk * 64, 64), :])
            UN[k, rows(chunk * 64, 64), :] = unit
            IV[k, rows(chunk * 64, 64), :] = jnp.broadcast_to(inverse, (64, 128))
            acted = gelu(unit * gain).astype(BF16)
            D[rows(chunk * 64, 64), :] = acted.astype(F32)
            put(chunk, acted.astype(F32))

    def turn(k):
        AT[k] = D[...].T.astype(BF16)

    def kernel_gradient(k, step):
        found = sources(step, -1)
        for first in (0, 2, 4, 6, 8):
            pair = found[first : first + 2]
            right = jnp.concatenate([ref[pl.ds(start, CELLS), :] for ref, start in pair], axis=1)
            both = jnp.dot(AT[k], right, preferred_element_type=F32)
            for n in range(len(pair)):
                for p in range(3):
                    G[p, pl.ds((first + n) * CH, CH), :] = both[:, n * CH + p * 128 : n * CH + (p + 1) * 128]

    def plane_send(slot):
        @pl.loop(1, 32)
        def _(step):
            q = (me + step) & 31
            pltpu.make_async_remote_copy(
                src_ref=AS.at[slot, rows(q * 16, 16)],
                dst_ref=AL.at[slot, rows(me * 16, 16)],
                send_sem=as_sem.at[slot],
                recv_sem=ar_sem.at[slot],
                device_id=plane(q),
                device_id_type=MESH,
            ).start()

        AL[slot, rows(me * 16, 16), :] = AS[slot, rows(me * 16, 16), :]

    def plane_wait(slot, sem):
        part = AL.at[slot, pl.ds(0, 31 * 16)]
        pltpu.make_async_copy(part, part, sem.at[slot]).wait()

    def plane_sent(slot):
        plane_wait(slot, as_sem)

    def to_far(slot, load, now=True):
        @pl.loop(0, 32, unroll=4)
        def _(q):
            both = jnp.concatenate([load(rows(q * 8, 8, 8)), load(rows(q * 8 + 256, 8, 8))], axis=0)
            AS[slot, rows(q * 16, 16), :] = both.astype(BF16)

        if now:
            plane_send(slot)

    def at_far(slot, store):
        plane_wait(slot, ar_sem)

        @pl.loop(0, 32, unroll=4)
        def _(q):
            both = AL[slot, rows(q * 16, 16), :].astype(F32)
            base = ((q >> 3) * 16 + (q & 7)) * 8
            store(rows(base, 8, 8), both[0:8])
            store(rows(base + 64, 8, 8), both[8:16])

    def to_near(slot, load):
        @pl.loop(0, 32, unroll=4)
        def _(q):
            base = ((q >> 3) * 16 + (q & 7)) * 8
            both = jnp.concatenate([load(rows(base, 8, 8)), load(rows(base + 64, 8, 8))], axis=0)
            AS[slot, rows(q * 16, 16), :] = both.astype(BF16)

        plane_send(slot)

    def at_near(slot, store):
        plane_wait(slot, ar_sem)

        @pl.loop(0, 32, unroll=4)
        def _(q):
            both = AL[slot, rows(q * 16, 16), :].astype(F32)
            store(rows(q * 8, 8, 8), both[0:8])
            store(rows(q * 8 + 256, 8, 8), both[8:16])

    def sibling_copy(k, p):
        return pltpu.make_async_remote_copy(
            src_ref=SB.at[k % 3, p, rows((1 - core) * 2048, 2048)],
            dst_ref=R0.at[k, p],
            send_sem=rs_sem.at[k, p, 0],
            recv_sem=rr_sem.at[k, p, 0],
            device_id=(gx + 1 - 2 * core, gy),
            device_id_type=MESH,
        )

    def held(p, level):
        base, size = core * 64, 64
        for n in range(level):
            size = size // 4
            base = base + here[ORDERS[p][n]] * size
        return base, size

    def axis_copy(k, p, level, step):
        axis = ORDERS[p][level - 1]
        base, size = held(p, level - 1)
        size = size // 4
        to = (here[axis] + step) & 3
        if level == 2:
            source = SB.at[k % 3, p, rows((base + to * size) * 32, size * 32)]
        else:
            source = TB.at[k, p, rows(to * 32, 32)]
        return pltpu.make_async_remote_copy(
            src_ref=source,
            dst_ref=(L2 if level == 2 else L3).at[k, p, step - 1],
            send_sem=rs_sem.at[k, p, level * 3 + step],
            recv_sem=rr_sem.at[k, p, level * 3 + step],
            device_id=device(core, {**here, axis: to}),
            device_id_type=MESH,
        )

    HOPS = ((2, 0, 1), (2, 1, 3), (1, 1, 1), (3, 0, 3), (1, 0, 1), (3, 1, 3))

    def ring_copy(k, p, slot):
        axis = ORDERS[p][0]
        of, half, by = HOPS[slot]
        start = core * 2048 + ((here[axis] + of) & 3) * 512 + half * 256
        return pltpu.make_async_remote_copy(
            src_ref=SB.at[k % 3, p, rows(start, 256)],
            dst_ref=L1.at[k, p, slot],
            send_sem=rs_sem.at[k, p, 1 + slot],
            recv_sem=rr_sem.at[k, p, 1 + slot],
            device_id=device(core, {**here, axis: (here[axis] + by) & 3}),
            device_id_type=MESH,
        )

    def reduce_0(k):
        if k == 0:
            reduce_sent(3)

        @pl.loop(0, 2)
        def _(high):
            @pl.loop(0, 2)
            def _(half):
                @pl.loop(0, 2)
                def _(low):
                    @pl.loop(0, 2)
                    def _(pair):
                        first = (high * 4 + half * 2 + low) * 16 + pair * 8
                        for p in range(3):
                            eight = G.at[p, rows(first * CHUNK, 8 * CHUNK + 8, 8)]
                            for n in range(8):
                                at = {"x": n % 4, "z": pair * 2 + n // 4, "y": high * 2 + low}
                                a, b, c = (at[axis] for axis in ORDERS[p])
                                to = half * 64 + a * 16 + b * 4 + c
                                SB[k % 3, p, rows(to * 32, 32), :] = eight[pl.ds(CHUNK * n, 32), :].astype(BF16)

        for p in range(3):
            sibling_copy(k, p).start()

    def reduce_sent(k):
        for p in range(3):
            sibling_copy(k, p).wait_send()
            for slot in range(6):
                ring_copy(k, p, slot).wait_send()
            for level in (2, 3):
                for step in (1, 2, 3):
                    axis_copy(k, p, level, step).wait_send()

    def reduce_1(k):
        for p in range(3):
            sibling_copy(k, p).wait_recv()

            @pl.loop(0, 4)
            def _(i, p=p):
                own = rows(core * 2048 + i * 512, 512)
                SB[k % 3, p, own, :] = SB[k % 3, p, own, :] + R0[k, p, rows(i * 512, 512), :]

            for slot in range(4):
                ring_copy(k, p, slot).start()

    def reduce_via(k):
        for p in range(3):
            for slot in (0, 1):
                ring_copy(k, p, slot).wait_recv()
                of, half, _ = HOPS[4 + slot]
                own = rows(core * 2048 + ((here[ORDERS[p][0]] + of) & 3) * 512 + half * 256, 256)
                SB[k % 3, p, own, :] = SB[k % 3, p, own, :] + L1[k, p, slot]
                ring_copy(k, p, 4 + slot).start()

    def reduce_next(k, level):
        for p in range(3):
            base, size = held(p, level)
            if level == 1:
                for slot in (2, 3, 4, 5):
                    ring_copy(k, p, slot).wait_recv()
                for half, arrived in ((0, (3, 4)), (1, (2, 5))):
                    own = rows(base * 32 + half * 256, 256)
                    total = SB[k % 3, p, own, :].astype(F32)
                    for slot in arrived:
                        total = total + L1[k, p, slot].astype(F32)
                    SB[k % 3, p, own, :] = total.astype(BF16)
            else:
                for step in (1, 2, 3):
                    axis_copy(k, p, level, step).wait_recv()
                total = SB[k % 3, p, rows(base * 32, size * 32), :].astype(F32)
                for step in (1, 2, 3):
                    total = total + L2[k, p, step - 1].astype(F32)
                TB[k, p] = total

            for step in (2, 1, 3):
                axis_copy(k, p, level + 1, step).start()

    def reduce_last(k):
        for p in range(3):
            for step in (1, 2, 3):
                axis_copy(k, p, 3, step).wait_recv()
            total = TB[k, p, rows(here[ORDERS[p][2]] * 32, 32, 8), :]
            for step in (1, 2, 3):
                total = total + L3[k, p, step - 1]
            total = total * (1.0 / 256.0)
            for r in range(CHUNK):
                wg_out[k : k + 1, r * CH + p * 128 : r * CH + (p + 1) * 128] = total[r : r + 1]

    load_x.wait()

    @pl.loop(0, 8)
    def _(chunk):
        S[0, rows(chunk * 64, 64), :] = X[rows(chunk * 64, 64), :].astype(F32)

    act(0, 0, lambda chunk, values: near_put(1, chunk, values))
    pl.semaphore_wait(barrier, greeted)
    halo_send(0, 1)
    load_cot.wait()
    to_far(0, lambda at: CT[at, :], now=False)
    turn(0)
    loads[0].wait()
    halo_receive(0, 1)
    near_versions(1)

    def grow(slot):
        def finish(at, result):
            S[slot + 1, at, :] = S[slot, at, :] + result

        return finish

    convolve(0, 8, 1, grow(0))

    act(1, 1, lambda chunk, values: near_put(4, chunk, values))
    halo_send(1, 4)
    turn(1)
    loads[1].wait()
    halo_receive(1, 4)
    near_versions(4)
    convolve(1, 32, 1, grow(1))

    to_far(1, lambda at: S[2, at, :])
    loads[2].wait()
    loads[3].wait()

    @pl.loop(0, 8)
    def _(i):
        pad_put(rows(i * 128, 32, 8), jnp.zeros((32, CH), F32))
        pad_put(rows(i * 128 + 96, 32, 8), jnp.zeros((32, CH), F32))

    def store_stream(at, values):
        S[3, at, :] = values

    at_far(1, store_stream)
    plane_send(0)

    act(2, 3, far_put)
    far_versions(1)
    convolve(2, 64, 1, grow(3))
    turn(2)
    act(3, 4, far_put)
    far_versions(4)

    def keep_updates(at, result):
        S[5, at, :] = (S[4, at, :] - S[3, at, :]) + result

    convolve(3, 256, 1, keep_updates)
    to_near(2, lambda at: S[5, at, :])
    turn(3)

    def store_gradient(at, values):
        S[6, at, :] = values

    at_far(0, store_gradient)

    def put_gradient(slot, put):
        @pl.loop(0, 8, unroll=4)
        def _(chunk):
            put(chunk, S[slot, rows(chunk * 64, 64), :].astype(BF16).astype(F32))

    def keep_d_act(at, result):
        D[at, :] = result

    def pull(k, finish):
        gain = gains[k : k + 1, :]

        @pl.loop(0, 8, unroll=4)
        def _(chunk):
            at = rows(chunk * 64, 64)
            finish(chunk, at, pulled(UN[k, at, :], IV[k, at, :][:, :1], gain, D[at, :]))

    put_gradient(6, far_put)
    far_versions(4)
    kernel_gradient(3, 256)
    reduce_0(3)
    convolve(3, 256, -1, keep_d_act)

    def far_3(chunk, at, pulled_back):
        S[5, at, :] = pulled_back
        S[6, at, :] = S[6, at, :] + pulled_back

    pull(3, far_3)
    reduce_1(3)
    put_gradient(6, far_put)
    far_versions(1)
    convolve(2, 64, -1, keep_d_act)

    def far_2(chunk, at, pulled_back):
        S[5, at, :] = S[5, at, :] + pulled_back

    pull(2, far_2)
    to_near(3, lambda at: S[5, at, :])
    reduce_via(3)
    kernel_gradient(2, 64)
    reduce_0(2)

    def store_output(at, values):
        S[2, at, :] = (S[2, at, :] - S[0, at, :]) + values

    at_near(2, store_output)
    save_out = pltpu.make_async_copy(S.at[2], out, io_sem.at[2])
    save_out.start()

    def store_near_gradient(at, values):
        S[6, at, :] = CT[at, :] + values
        S[5, at, :] = values

    at_near(3, store_near_gradient)
    put_gradient(6, lambda chunk, values: near_put(4, chunk, values))
    halo_send(2, 4)
    reduce_next(3, 1)
    halo_receive(2, 4)
    near_versions(4)
    reduce_1(2)
    convolve(1, 32, -1, keep_d_act)

    def near_1(chunk, at, pulled_back):
        total = S[6, at, :] + pulled_back
        S[5, at, :] = S[5, at, :] + pulled_back
        near_put(1, chunk, total.astype(BF16).astype(F32))

    pull(1, near_1)
    halo_send(3, 1)
    reduce_next(3, 2)
    reduce_via(2)
    kernel_gradient(1, 32)
    reduce_0(1)
    reduce_next(2, 1)
    halo_receive(3, 1)
    near_versions(1)
    kernel_gradient(0, 8)
    reduce_1(1)
    reduce_last(3)
    reduce_0(0)
    convolve(0, 8, -1, keep_d_act)

    def near_0(chunk, at, pulled_back):
        S[5, at, :] = S[5, at, :] + pulled_back

    reduce_via(1)
    reduce_next(2, 2)
    reduce_1(0)
    pull(0, near_0)
    save_ig = pltpu.make_async_copy(S.at[5], ig, io_sem.at[3])
    save_ig.start()
    reduce_next(1, 1)
    reduce_via(0)
    reduce_last(2)
    reduce_next(1, 2)
    reduce_next(0, 1)
    reduce_last(1)
    reduce_next(0, 2)
    reduce_last(0)

    save_out.wait()
    save_ig.wait()

    for k in (2, 1, 0):
        reduce_sent(k)
    for slot in range(4):
        plane_sent(slot)
    for slot, d in enumerate((1, 4, 4, 1)):
        halo_sent(slot, d)


def closing(x_ref, grown, cot_ref, pulled_back, shares, out, ig, wg):
    out[...] = x_ref[...].astype(F32) + grown[...]
    ig[...] = cot_ref[...] + pulled_back[...]

    @pl.when(pl.program_id(0) == 0)
    def _():
        wg[...] = shares[...]


def body(inputs, norm_gains, weights, cotangent):
    vmem = pl.BlockSpec(memory_space=pltpu.VMEM)
    hbm = pl.BlockSpec(memory_space=pl.ANY)
    out, input_grad, shares = pl.pallas_call(
        kernel,
        out_shape=(
            jax.ShapeDtypeStruct((CELLS, CH), F32),
            jax.ShapeDtypeStruct((CELLS, CH), F32),
            jax.ShapeDtypeStruct((4, CHUNK * CH), F32),
        ),
        in_specs=[hbm, vmem, hbm, hbm],
        out_specs=(hbm, hbm, vmem),
        scratch_shapes=[
            pltpu.VMEM((4, 9 * CH, CH), BF16),
            pltpu.VMEM((CELLS, CH), BF16),
            pltpu.VMEM((CELLS, CH), F32),
            pltpu.VMEM((7, CELLS, CH), F32),
            pltpu.VMEM((CELLS, CH), F32),
            pltpu.VMEM((4, CELLS, CH), F32),
            pltpu.VMEM((4, CELLS, 128), F32),
            pltpu.VMEM((4, CH, CELLS), BF16),
            pltpu.VMEM((3, 72 * PITCH, 128), F32),
            pltpu.VMEM((3, 1024, CH), BF16),
            pltpu.VMEM((3, CELLS, CH), BF16),
            pltpu.VMEM((3, 9 * CH + 8, 128), F32),
            pltpu.VMEM((3, 3, 4096, 128), BF16),
            pltpu.VMEM((4, 3, 128, 128), F32),
            pltpu.VMEM((4, 3, 2048, 128), BF16),
            pltpu.VMEM((4, 3, 6, 256, 128), BF16),
            pltpu.VMEM((4, 3, 3, 128, 128), BF16),
            pltpu.VMEM((4, 3, 3, 32, 128), F32),
            pltpu.VMEM((4, CELLS, CH), BF16),
            pltpu.VMEM((4, CELLS, CH), BF16),
            pltpu.VMEM((4, 576, CH), BF16),
            pltpu.VMEM((4, 704, CH), BF16),
            pltpu.SemaphoreType.DMA((4,)),
            pltpu.SemaphoreType.DMA((4,)),
            pltpu.SemaphoreType.DMA((4, 8)),
            pltpu.SemaphoreType.DMA((4, 8)),
            pltpu.SemaphoreType.DMA((4,)),
            pltpu.SemaphoreType.DMA((4,)),
            pltpu.SemaphoreType.DMA((4, 3, 13)),
            pltpu.SemaphoreType.DMA((4, 3, 13)),
        ],
        compiler_params=pltpu.CompilerParams(
            collective_id=0, has_side_effects=True, vmem_limit_bytes=64 * 1024 * 1024
        ),
        cost_estimate=pl.CostEstimate(flops=16_300_000_000, bytes_accessed=15_000_000, transcendentals=4_000_000),
    )(inputs.reshape(CELLS, CH), norm_gains, weights, cotangent.reshape(CELLS, CH))
    part = pl.BlockSpec((CELLS // 4, CH), lambda i: (i, 0))
    whole = pl.BlockSpec((4, CHUNK * CH), lambda i: (0, 0))
    out, input_grad, shares = pl.pallas_call(
        closing,
        grid=(4,),
        out_shape=(
            jax.ShapeDtypeStruct((CELLS, CH), F32),
            jax.ShapeDtypeStruct((CELLS, CH), F32),
            jax.ShapeDtypeStruct((4, CHUNK * CH), F32),
        ),
        in_specs=[part, part, part, part, whole],
        out_specs=(part, part, whole),
        cost_estimate=pl.CostEstimate(flops=400_000, bytes_accessed=4_600_000, transcendentals=0),
    )(inputs.reshape(CELLS, CH), out, cotangent.reshape(CELLS, CH), input_grad, shares)
    shape = (ROWS, COLS, CH)
    return out.reshape(shape), input_grad.reshape(shape), shares


def solution(mesh):
    placed = (P("gx", "gy", None), P(), P(), P("gx", "gy", None))
    return jax.shard_map(
        body,
        mesh=mesh,
        in_specs=placed,
        out_specs=(P("gx", "gy", None), P("gx", "gy", None), P(None, ("gx", "gy"))),
        check_vma=False,
    )
```

```python
import math

import jax
import jax.numpy as jnp
from jax import lax
from jax.experimental import pallas as pl
from jax.experimental.pallas import tpu as pltpu
from jax.sharding import PartitionSpec as P

F32 = jnp.float32
BF16 = jnp.bfloat16
MESH = pl.DeviceIdType.MESH
CH = 384
ROWS, COLS = 64, 8
CELLS = ROWS * COLS
TAPS = tuple((r, c) for r in (-1, 0, 1) for c in (-1, 0, 1))
EPSILON = 1e-05
ROOT = math.sqrt(2.0 / math.pi)
CUBIC = 0.044715
PITCH = 24
DIRS = ((0, -1), (0, 1), (-1, 0), (1, 0), (-1, -1), (-1, 1), (1, -1), (1, 1))
CHUNK = 27
ORDERS = (("x", "y", "z"), ("y", "z", "x"), ("z", "x", "y"))


def aligned(value, step):
    return value if isinstance(value, int) else pl.multiple_of(value, step)


def rows(start, size, step=16):
    return pl.ds(aligned(start, step), size)


def normed(stream):
    average = jnp.mean(stream, axis=-1, keepdims=True)
    centred = stream - average
    spread = jnp.mean(centred * centred, axis=-1, keepdims=True)
    inverse = lax.rsqrt(spread + EPSILON)
    return centred * inverse, inverse


def gelu(u):
    half = 0.5 * u
    return half + half * jnp.tanh(u * (ROOT + (ROOT * CUBIC) * (u * u)))


def gelu_slope(u):
    square = u * u
    t = jnp.tanh(u * (ROOT + (ROOT * CUBIC) * square))
    rest = (1.0 - t) * u * (ROOT + (3.0 * ROOT * CUBIC) * square)
    return (0.5 + 0.5 * t) * (1.0 + rest)


def pulled(unit, inverse, gain, d_act):
    d_unit = d_act * gelu_slope(unit * gain) * gain
    first = jnp.mean(d_unit, axis=-1, keepdims=True)
    second = jnp.mean(d_unit * unit, axis=-1, keepdims=True)
    return inverse * (d_unit - first - unit * second)


def strip_rows(d):
    return (ROWS * d, ROWS * d, max(COLS * d, 16), max(COLS * d, 16))


def kernel(
    x_hbm, gains, w_hbm, cot_hbm, out, ig, wg_out,
    W, X, CT, S, D, UN, IV, AT, F, V, U, G, SB, TB, R0, L1, L2, L3, AS, AL, HS, HL,
    w_sem, io_sem, hs_sem, hr_sem, as_sem, ar_sem, rs_sem, rr_sem,
):
    gx, gy = lax.axis_index("gx"), lax.axis_index("gy")
    core, y = gx & 1, (gx >> 1) * 2 + (gy >> 4)
    z, x = (gy >> 2) & 3, gy & 3
    here = {"x": x, "y": y, "z": z}
    me = gx * 8 + (gy >> 2)

    def device(core_of, at):
        return ((at["y"] >> 1) * 2 + core_of, (at["y"] & 1) * 16 + at["z"] * 4 + at["x"])

    def plane(q):
        return (q >> 3, (q & 7) * 4 + x)

    def exists(direction):
        r, c = gx + direction[0], gy + direction[1]
        return (r >= 0) & (r < 4) & (c >= 0) & (c < 32)

    barrier = pltpu.get_barrier_semaphore()

    def greet(target):
        pl.semaphore_signal(barrier, inc=1, device_id=target, device_id_type=MESH)

    @pl.loop(1, 32)
    def _(step):
        greet(plane((me + step) & 31))

    for step in (1, 2, 3):
        greet(device(core, {**here, "x": (x + step) & 3}))
    greeted = 34
    for direction in DIRS:
        there = exists(direction)

        @pl.when(there)
        def _(direction=direction):
            greet((gx + direction[0], gy + direction[1]))

        greeted = greeted + there.astype(jnp.int32)

    load_x = pltpu.make_async_copy(x_hbm, X, io_sem.at[0])
    load_x.start()
    load_cot = pltpu.make_async_copy(cot_hbm, CT, io_sem.at[1])
    load_cot.start()
    loads = []
    for k in range(4):
        loads.append(pltpu.make_async_copy(w_hbm.at[k], W.at[k], w_sem.at[k]))
        loads[k].start()

    def padded(at):
        return jnp.concatenate([F[p, at, :] for p in range(3)], axis=1)

    def pad_put(at, values):
        for p in range(3):
            F[p, at, :] = values[:, p * 128 : (p + 1) * 128]

    def halo_copy(slot, d, index):
        sizes = strip_rows(d)
        source = (0, 1, 2, 3, 2, 2, 3, 3)[index]
        size = sizes[source]
        starts = [sum(sizes[:i]) for i in range(4)]
        landed = (0, 1, 2, 3, 2, 2, 3, 3)
        lands = [sum(sizes[landed[j]] for j in range(i)) for i in range(8)]
        direction = DIRS[index]
        opposite = DIRS.index((-direction[0], -direction[1]))
        return pltpu.make_async_remote_copy(
            src_ref=HS.at[slot, pl.ds(starts[source], size)],
            dst_ref=HL.at[slot, pl.ds(lands[opposite], size)],
            send_sem=hs_sem.at[slot, index],
            recv_sem=hr_sem.at[slot, opposite],
            device_id=(gx + direction[0], gy + direction[1]),
            device_id_type=MESH,
        )

    def halo_send(slot, d):
        sizes = strip_rows(d)
        at = 0
        for first in (0, COLS - d):
            for j in range(d):
                column = padded(pl.ds(d * PITCH + 8 + first + j, ROWS, stride=PITCH))
                HS[slot, pl.ds(at + j * ROWS, ROWS), :] = column.astype(BF16)
            at += ROWS * d
        count = sizes[2] // COLS
        for first in (0, ROWS - count):
            for i in range(0, count, 2):
                pair = [padded(pl.ds((d + first + i + n) * PITCH + 8, 8)) for n in (0, 1)]
                HS[slot, pl.ds(at + i * 8, 16), :] = jnp.concatenate(pair, axis=0).astype(BF16)
            at += sizes[2]
        for index, direction in enumerate(DIRS):

            @pl.when(exists(direction))
            def _(index=index):
                halo_copy(slot, d, index).start()

    def halo_sent(slot, d):
        for index, direction in enumerate(DIRS):

            @pl.when(exists(direction))
            def _(index=index):
                halo_copy(slot, d, index).wait_send()

    def halo_receive(slot, d):
        sizes = strip_rows(d)
        landed = (0, 1, 2, 3, 2, 2, 3, 3)
        lands = [sum(sizes[landed[j]] for j in range(i)) for i in range(8)]
        count = sizes[2] // COLS
        for index, direction in enumerate(DIRS):
            there = exists(direction)

            def put(values, index=index, direction=direction):
                if direction[0] == 0:
                    first = 8 - d if direction[1] < 0 else 16
                    for j in range(d):
                        pad_put(pl.ds(d * PITCH + first + j, ROWS, stride=PITCH), values(j * ROWS, ROWS))
                else:
                    first = 0 if direction[0] < 0 else d + ROWS
                    skip = count - d if direction[0] < 0 else 0
                    for i in range(0, count, 2):
                        both = values(i * 8, 16)
                        for n in (0, 1):
                            row = i + n - skip
                            if 0 <= row < d:
                                start = (first + row) * PITCH + 8 + 8 * direction[1]
                                pad_put(pl.ds(start, 8), both[n * 8 : n * 8 + 8])

            @pl.when(there)
            def _(index=index, direction=direction, put=put):
                opposite = DIRS.index((-direction[0], -direction[1]))
                halo_copy(slot, d, opposite).wait_recv()
                put(lambda at, size: HL[slot, pl.ds(lands[index] + at, size), :].astype(F32))

            @pl.when(jnp.logical_not(there))
            def _(put=put):
                put(lambda at, size: jnp.zeros((size, CH), F32))

    def near_versions(d):
        @pl.loop(0, (ROWS + 2 * d) // 2, unroll=3 if d == 1 else 4)
        def _(i):
            pair = [padded(rows((2 * i + n) * PITCH, PITCH, 8)) for n in (0, 1)]
            for c in (-1, 0, 1):
                both = [row[8 + c * d : 16 + c * d] for row in pair]
                V[c + 1, rows(i * 16, 16), :] = jnp.concatenate(both, axis=0).astype(BF16)

        if d == 1:

            @pl.loop(0, ROWS // 2, unroll=4)
            def _(i):
                pair = [padded(rows((2 * i + n + 1) * PITCH, PITCH, 8)) for n in (0, 1)]
                for c in (-1, 0, 1):
                    both = [row[8 + c * d : 16 + c * d] for row in pair]
                    U[c + 1, rows(i * 16, 16), :] = jnp.concatenate(both, axis=0).astype(BF16)

    def near_put(d, chunk, values):
        for i in range(8):
            pad_put(rows((d + chunk * 8 + i) * PITCH + 8, 8, 8), values[i * 8 : i * 8 + 8])

    def far_put(chunk, values):
        pad_put(rows(chunk * 128 + 32, 64, 8), values)

    def far_versions(s):
        for c in (-1, 0, 1):
            if s == 1:
                V[c + 1, pl.ds(0, 64), :] = jnp.zeros((64, CH), BF16)
                V[c + 1, pl.ds(576, 64), :] = jnp.zeros((64, CH), BF16)

            @pl.loop(0, 8, unroll=4)
            def _(i, c=c):
                V[c + 1, rows((i + s) * 64, 64), :] = padded(rows(i * 128 + 32 + c * s * 8, 64, 8)).astype(BF16)

    def sources(step, sign):
        found = []
        for r, c in TAPS:
            r, c = sign * r, sign * c
            if step == 8 and r == 0:
                found.append((U.at[c + 1], 0))
            else:
                found.append((V.at[c + 1], (1 + r) * step))
        return found

    def convolve(k, step, sign, finish):
        found = sources(step, sign)
        pieces = ((0, CELLS, 0, 9),)
        if k == 3:
            pieces = ((0, 256, 3, 9), (256, 256, 0, 6)) if sign == 1 else ((0, 256, 0, 6), (256, 256, 3, 9))
        for at, size, first, last in pieces:
            left = jnp.concatenate([ref[pl.ds(at + start, size), :] for ref, start in found[first:last]], axis=1)
            if sign == 1:
                result = jnp.dot(left, W[k, first * CH : last * CH, :], preferred_element_type=F32)
            else:
                right = jnp.concatenate([W[k, t * CH : (t + 1) * CH, :] for t in range(first, last)], axis=1)
                result = lax.dot_general(left, right, (((1,), (1,)), ((), ())), preferred_element_type=F32)
            finish(pl.ds(at, size), result)

    def act(k, slot, put):
        gain = gains[k : k + 1, :]

        @pl.loop(0, 8, unroll=8)
        def _(chunk):
            unit, inverse = normed(S[slot, rows(chunk * 64, 64), :])
            UN[k, rows(chunk * 64, 64), :] = unit
            IV[k, rows(chunk * 64, 64), :] = jnp.broadcast_to(inverse, (64, 128))
            acted = gelu(unit * gain).astype(BF16)
            D[rows(chunk * 64, 64), :] = acted.astype(F32)
            put(chunk, acted.astype(F32))

    def turn(k):
        AT[k] = D[...].T.astype(BF16)

    def kernel_gradient(k, step):
        found = sources(step, -1)
        groups = tuple((first, 2, 0, CELLS) for first in (0, 2, 4, 6)) + ((8, 1, 0, CELLS),)
        if k == 3:
            groups = ((0, 2, 0, 256), (2, 1, 0, 256), (3, 2, 0, CELLS), (5, 1, 0, CELLS), (6, 2, 256, 256), (8, 1, 256, 256))
        for first, count, at, size in groups:
            taps = found[first : first + count]
            right = jnp.concatenate([ref[pl.ds(at + start, size), :] for ref, start in taps], axis=1)
            both = jnp.dot(AT[k, :, at : at + size], right, preferred_element_type=F32)
            for n in range(count):
                for p in range(3):
                    G[p, pl.ds((first + n) * CH, CH), :] = both[:, n * CH + p * 128 : n * CH + (p + 1) * 128]

    def plane_send(slot):
        @pl.loop(1, 32)
        def _(step):
            q = (me + step) & 31
            pltpu.make_async_remote_copy(
                src_ref=AS.at[slot, rows(q * 16, 16)],
                dst_ref=AL.at[slot, rows(me * 16, 16)],
                send_sem=as_sem.at[slot],
                recv_sem=ar_sem.at[slot],
                device_id=plane(q),
                device_id_type=MESH,
            ).start()

        AL[slot, rows(me * 16, 16), :] = AS[slot, rows(me * 16, 16), :]

    def plane_wait(slot, sem):
        part = AL.at[slot, pl.ds(0, 31 * 16)]
        pltpu.make_async_copy(part, part, sem.at[slot]).wait()

    def plane_sent(slot):
        plane_wait(slot, as_sem)

    def to_far(slot, load, now=True):
        @pl.loop(0, 32, unroll=4)
        def _(q):
            both = jnp.concatenate([load(rows(q * 8, 8, 8)), load(rows(q * 8 + 256, 8, 8))], axis=0)
            AS[slot, rows(q * 16, 16), :] = both.astype(BF16)

        if now:
            plane_send(slot)

    def at_far(slot, store):
        plane_wait(slot, ar_sem)

        @pl.loop(0, 32, unroll=4)
        def _(q):
            both = AL[slot, rows(q * 16, 16), :].astype(F32)
            base = ((q >> 3) * 16 + (q & 7)) * 8
            store(rows(base, 8, 8), both[0:8])
            store(rows(base + 64, 8, 8), both[8:16])

    def to_near(slot, load):
        @pl.loop(0, 32, unroll=4)
        def _(q):
            base = ((q >> 3) * 16 + (q & 7)) * 8
            both = jnp.concatenate([load(rows(base, 8, 8)), load(rows(base + 64, 8, 8))], axis=0)
            AS[slot, rows(q * 16, 16), :] = both.astype(BF16)

        plane_send(slot)

    def at_near(slot, store):
        plane_wait(slot, ar_sem)

        @pl.loop(0, 32, unroll=4)
        def _(q):
            both = AL[slot, rows(q * 16, 16), :].astype(F32)
            store(rows(q * 8, 8, 8), both[0:8])
            store(rows(q * 8 + 256, 8, 8), both[8:16])

    def sibling_copy(k, p):
        return pltpu.make_async_remote_copy(
            src_ref=SB.at[k % 3, p, rows((1 - core) * 2048, 2048)],
            dst_ref=R0.at[k, p],
            send_sem=rs_sem.at[k, p, 0],
            recv_sem=rr_sem.at[k, p, 0],
            device_id=(gx + 1 - 2 * core, gy),
            device_id_type=MESH,
        )

    def held(p, level):
        base, size = core * 64, 64
        for n in range(level):
            size = size // 4
            base = base + here[ORDERS[p][n]] * size
        return base, size

    def axis_copy(k, p, level, step):
        axis = ORDERS[p][level - 1]
        base, size = held(p, level - 1)
        size = size // 4
        to = (here[axis] + step) & 3
        if level == 2:
            source = SB.at[k % 3, p, rows((base + to * size) * 32, size * 32)]
        else:
            source = TB.at[k, p, rows(to * 32, 32)]
        return pltpu.make_async_remote_copy(
            src_ref=source,
            dst_ref=(L2 if level == 2 else L3).at[k, p, step - 1],
            send_sem=rs_sem.at[k, p, level * 3 + step],
            recv_sem=rr_sem.at[k, p, level * 3 + step],
            device_id=device(core, {**here, axis: to}),
            device_id_type=MESH,
        )

    HOPS = ((2, 0, 1), (2, 1, 3), (1, 1, 1), (3, 0, 3), (1, 0, 1), (3, 1, 3))

    def ring_copy(k, p, slot):
        axis = ORDERS[p][0]
        of, half, by = HOPS[slot]
        start = core * 2048 + ((here[axis] + of) & 3) * 512 + half * 256
        return pltpu.make_async_remote_copy(
            src_ref=SB.at[k % 3, p, rows(start, 256)],
            dst_ref=L1.at[k, p, slot],
            send_sem=rs_sem.at[k, p, 1 + slot],
            recv_sem=rr_sem.at[k, p, 1 + slot],
            device_id=device(core, {**here, axis: (here[axis] + by) & 3}),
            device_id_type=MESH,
        )

    def reduce_0(k):
        if k == 0:
            reduce_sent(3)

        @pl.loop(0, 2)
        def _(high):
            @pl.loop(0, 2)
            def _(half):
                @pl.loop(0, 2)
                def _(low):
                    @pl.loop(0, 2, unroll=2)
                    def _(pair):
                        first = (high * 4 + half * 2 + low) * 16 + pair * 8
                        for p in range(3):
                            eight = G.at[p, rows(first * CHUNK, 8 * CHUNK + 8, 8)]
                            for n in range(8):
                                at = {"x": n % 4, "z": pair * 2 + n // 4, "y": high * 2 + low}
                                a, b, c = (at[axis] for axis in ORDERS[p])
                                to = half * 64 + a * 16 + b * 4 + c
                                SB[k % 3, p, rows(to * 32, 32), :] = eight[pl.ds(CHUNK * n, 32), :].astype(BF16)

        for p in range(3):
            sibling_copy(k, p).start()

    def reduce_sent(k):
        for p in range(3):
            sibling_copy(k, p).wait_send()
            for slot in range(6):
                ring_copy(k, p, slot).wait_send()
            for level in (2, 3):
                for step in (1, 2, 3):
                    axis_copy(k, p, level, step).wait_send()

    def reduce_1(k):
        for p in range(3):
            sibling_copy(k, p).wait_recv()

            @pl.loop(0, 4)
            def _(i, p=p):
                own = rows(core * 2048 + i * 512, 512)
                SB[k % 3, p, own, :] = SB[k % 3, p, own, :] + R0[k, p, rows(i * 512, 512), :]

            for slot in range(4):
                ring_copy(k, p, slot).start()

    def reduce_via(k):
        for p in range(3):
            for slot in (0, 1):
                ring_copy(k, p, slot).wait_recv()
                of, half, _ = HOPS[4 + slot]
                own = rows(core * 2048 + ((here[ORDERS[p][0]] + of) & 3) * 512 + half * 256, 256)
                SB[k % 3, p, own, :] = SB[k % 3, p, own, :] + L1[k, p, slot]
                ring_copy(k, p, 4 + slot).start()

    def reduce_next(k, level):
        for p in range(3):
            base, size = held(p, level)
            if level == 1:
                for slot in (2, 3, 4, 5):
                    ring_copy(k, p, slot).wait_recv()
                for half, arrived in ((0, (3, 4)), (1, (2, 5))):
                    own = rows(base * 32 + half * 256, 256)
                    total = SB[k % 3, p, own, :].astype(F32)
                    for slot in arrived:
                        total = total + L1[k, p, slot].astype(F32)
                    SB[k % 3, p, own, :] = total.astype(BF16)
            else:
                for step in (1, 2, 3):
                    axis_copy(k, p, level, step).wait_recv()
                total = SB[k % 3, p, rows(base * 32, size * 32), :].astype(F32)
                for step in (1, 2, 3):
                    total = total + L2[k, p, step - 1].astype(F32)
                TB[k, p] = total

            for step in (2, 1, 3):
                axis_copy(k, p, level + 1, step).start()

    def reduce_last(k):
        for p in range(3):
            for step in (1, 2, 3):
                axis_copy(k, p, 3, step).wait_recv()
            total = TB[k, p, rows(here[ORDERS[p][2]] * 32, 32, 8), :]
            for step in (1, 2, 3):
                total = total + L3[k, p, step - 1]
            total = total * (1.0 / 256.0)
            for r in range(CHUNK):
                wg_out[k : k + 1, r * CH + p * 128 : r * CH + (p + 1) * 128] = total[r : r + 1]

    load_x.wait()

    @pl.loop(0, 8)
    def _(chunk):
        S[0, rows(chunk * 64, 64), :] = X[rows(chunk * 64, 64), :].astype(F32)

    act(0, 0, lambda chunk, values: near_put(1, chunk, values))
    pl.semaphore_wait(barrier, greeted)
    halo_send(0, 1)
    load_cot.wait()
    to_far(0, lambda at: CT[at, :], now=False)
    turn(0)
    loads[0].wait()
    halo_receive(0, 1)
    near_versions(1)

    def grow(slot):
        def finish(at, result):
            S[slot + 1, at, :] = S[slot, at, :] + result

        return finish

    convolve(0, 8, 1, grow(0))

    act(1, 1, lambda chunk, values: near_put(4, chunk, values))
    halo_send(1, 4)
    turn(1)
    loads[1].wait()
    halo_receive(1, 4)
    near_versions(4)
    convolve(1, 32, 1, grow(1))

    to_far(1, lambda at: S[2, at, :])
    loads[2].wait()
    loads[3].wait()

    @pl.loop(0, 8)
    def _(i):
        pad_put(rows(i * 128, 32, 8), jnp.zeros((32, CH), F32))
        pad_put(rows(i * 128 + 96, 32, 8), jnp.zeros((32, CH), F32))

    def store_stream(at, values):
        S[3, at, :] = values

    at_far(1, store_stream)
    plane_send(0)

    act(2, 3, far_put)
    far_versions(1)
    convolve(2, 64, 1, grow(3))
    turn(2)
    act(3, 4, far_put)
    far_versions(4)

    def keep_updates(at, result):
        S[5, at, :] = (S[4, at, :] - S[3, at, :]) + result

    convolve(3, 256, 1, keep_updates)
    to_near(2, lambda at: S[5, at, :])
    turn(3)

    def store_gradient(at, values):
        S[1, at, :] = values

    at_far(0, store_gradient)

    def put_gradient(slot, put):
        @pl.loop(0, 8, unroll=4)
        def _(chunk):
            put(chunk, S[slot, rows(chunk * 64, 64), :].astype(BF16).astype(F32))

    def keep_d_act(at, result):
        D[at, :] = result

    def pull(k, finish):
        gain = gains[k : k + 1, :]

        @pl.loop(0, 8, unroll=8)
        def _(chunk):
            at = rows(chunk * 64, 64)
            finish(chunk, at, pulled(UN[k, at, :], IV[k, at, :][:, :1], gain, D[at, :]))

    put_gradient(1, far_put)
    far_versions(4)
    kernel_gradient(3, 256)
    reduce_0(3)
    convolve(3, 256, -1, keep_d_act)

    def far_3(chunk, at, pulled_back):
        S[5, at, :] = pulled_back
        S[1, at, :] = S[1, at, :] + pulled_back

    pull(3, far_3)
    reduce_1(3)
    put_gradient(1, far_put)
    far_versions(1)
    convolve(2, 64, -1, keep_d_act)

    def far_2(chunk, at, pulled_back):
        S[5, at, :] = S[5, at, :] + pulled_back

    pull(2, far_2)
    to_near(3, lambda at: S[5, at, :])
    reduce_via(3)
    kernel_gradient(2, 64)
    reduce_0(2)

    def store_output(at, values):
        S[2, at, :] = (S[2, at, :] - S[0, at, :]) + values

    at_near(2, store_output)
    save_out = pltpu.make_async_copy(S.at[2], out, io_sem.at[2])
    save_out.start()

    def store_near_gradient(at, values):
        S[1, at, :] = CT[at, :] + values
        S[5, at, :] = values

    at_near(3, store_near_gradient)
    put_gradient(1, lambda chunk, values: near_put(4, chunk, values))
    halo_send(2, 4)
    reduce_next(3, 1)
    halo_receive(2, 4)
    near_versions(4)
    reduce_1(2)
    convolve(1, 32, -1, keep_d_act)

    def near_1(chunk, at, pulled_back):
        total = S[1, at, :] + pulled_back
        S[5, at, :] = S[5, at, :] + pulled_back
        near_put(1, chunk, total.astype(BF16).astype(F32))

    pull(1, near_1)
    halo_send(3, 1)
    reduce_next(3, 2)
    reduce_via(2)
    kernel_gradient(1, 32)
    reduce_0(1)
    reduce_next(2, 1)
    halo_receive(3, 1)
    near_versions(1)
    kernel_gradient(0, 8)
    reduce_1(1)
    reduce_last(3)
    reduce_0(0)
    convolve(0, 8, -1, keep_d_act)

    def near_0(chunk, at, pulled_back):
        S[5, at, :] = S[5, at, :] + pulled_back

    reduce_via(1)
    reduce_next(2, 2)
    reduce_1(0)
    pull(0, near_0)
    save_ig = pltpu.make_async_copy(S.at[5], ig, io_sem.at[3])
    save_ig.start()
    reduce_next(1, 1)
    reduce_via(0)
    reduce_last(2)
    reduce_next(1, 2)
    reduce_next(0, 1)
    reduce_last(1)
    reduce_next(0, 2)
    reduce_last(0)

    save_out.wait()
    save_ig.wait()

    for k in (2, 1, 0):
        reduce_sent(k)
    for slot in range(4):
        plane_sent(slot)
    for slot, d in enumerate((1, 4, 4, 1)):
        halo_sent(slot, d)


def closing(x_ref, grown, cot_ref, pulled_back, shares, out, ig, wg):
    out[...] = x_ref[...].astype(F32) + grown[...]
    ig[...] = cot_ref[...] + pulled_back[...]

    @pl.when(pl.program_id(0) == 0)
    def _():
        wg[...] = shares[...]


def body(inputs, norm_gains, weights, cotangent):
    vmem = pl.BlockSpec(memory_space=pltpu.VMEM)
    hbm = pl.BlockSpec(memory_space=pl.ANY)
    out, input_grad, shares = pl.pallas_call(
        kernel,
        out_shape=(
            jax.ShapeDtypeStruct((CELLS, CH), F32),
            jax.ShapeDtypeStruct((CELLS, CH), F32),
            jax.ShapeDtypeStruct((4, CHUNK * CH), F32),
        ),
        in_specs=[hbm, vmem, hbm, hbm],
        out_specs=(hbm, hbm, vmem),
        scratch_shapes=[
            pltpu.VMEM((4, 9 * CH, CH), BF16),
            pltpu.VMEM((CELLS, CH), BF16),
            pltpu.VMEM((CELLS, CH), F32),
            pltpu.VMEM((6, CELLS, CH), F32),
            pltpu.VMEM((CELLS, CH), F32),
            pltpu.VMEM((4, CELLS, CH), F32),
            pltpu.VMEM((4, CELLS, 128), F32),
            pltpu.VMEM((4, CH, CELLS), BF16),
            pltpu.VMEM((3, 72 * PITCH, 128), F32),
            pltpu.VMEM((3, 1024, CH), BF16),
            pltpu.VMEM((3, CELLS, CH), BF16),
            pltpu.VMEM((3, 9 * CH + 8, 128), F32),
            pltpu.VMEM((3, 3, 4096, 128), BF16),
            pltpu.VMEM((4, 3, 128, 128), F32),
            pltpu.VMEM((4, 3, 2048, 128), BF16),
            pltpu.VMEM((4, 3, 6, 256, 128), BF16),
            pltpu.VMEM((4, 3, 3, 128, 128), BF16),
            pltpu.VMEM((4, 3, 3, 32, 128), F32),
            pltpu.VMEM((4, CELLS, CH), BF16),
            pltpu.VMEM((4, CELLS, CH), BF16),
            pltpu.VMEM((4, 576, CH), BF16),
            pltpu.VMEM((4, 704, CH), BF16),
            pltpu.SemaphoreType.DMA((4,)),
            pltpu.SemaphoreType.DMA((4,)),
            pltpu.SemaphoreType.DMA((4, 8)),
            pltpu.SemaphoreType.DMA((4, 8)),
            pltpu.SemaphoreType.DMA((4,)),
            pltpu.SemaphoreType.DMA((4,)),
            pltpu.SemaphoreType.DMA((4, 3, 13)),
            pltpu.SemaphoreType.DMA((4, 3, 13)),
        ],
        compiler_params=pltpu.CompilerParams(
            collective_id=0, has_side_effects=True, vmem_limit_bytes=64 * 1024 * 1024
        ),
        cost_estimate=pl.CostEstimate(flops=16_300_000_000, bytes_accessed=15_000_000, transcendentals=4_000_000),
    )(inputs.reshape(CELLS, CH), norm_gains, weights, cotangent.reshape(CELLS, CH))
    part = pl.BlockSpec((CELLS // 4, CH), lambda i: (i, 0))
    whole = pl.BlockSpec((4, CHUNK * CH), lambda i: (0, 0))
    out, input_grad, shares = pl.pallas_call(
        closing,
        grid=(4,),
        out_shape=(
            jax.ShapeDtypeStruct((CELLS, CH), F32),
            jax.ShapeDtypeStruct((CELLS, CH), F32),
            jax.ShapeDtypeStruct((4, CHUNK * CH), F32),
        ),
        in_specs=[part, part, part, part, whole],
        out_specs=(part, part, whole),
        cost_estimate=pl.CostEstimate(flops=400_000, bytes_accessed=4_600_000, transcendentals=0),
    )(inputs.reshape(CELLS, CH), out, cotangent.reshape(CELLS, CH), input_grad, shares)
    shape = (ROWS, COLS, CH)
    return out.reshape(shape), input_grad.reshape(shape), shares


def solution(mesh):
    placed = (P("gx", "gy", None), P(), P(), P("gx", "gy", None))
    return jax.shard_map(
        body,
        mesh=mesh,
        in_specs=placed,
        out_specs=(P("gx", "gy", None), P("gx", "gy", None), P(None, ("gx", "gy"))),
        check_vma=False,
    )
```
